512 devices in a mesh: lon: 64 (over z, x, core), lat: 8 (over y).
Axes of the slice: x: 4, y: 8, z: 8, core: 2. Of those that a mesh axis runs over, the one named last changes fastest.
Arguments:
- spec_pts: bfloat16 [36, 36, 262144], P(None, None, ('lon', 'lat')), may hold values from 0.049804688 to 2
- wind_u: float32 [262144], P(('lon', 'lat')), may hold values from -40 to 40
- wind_v: float32 [262144], P(('lon', 'lat')), may hold values from -40 to 40
- ocean_current: bfloat16 [2, 8, 512, 128], P(None, 'lat', 'lon'), may hold values from -0.099609375 to 0.099609375
- block_owner: int32 [32, 64], P('lat', 'lon'), may hold values from 0 to 63, as said below
- block_slot: int32 [32, 64], P('lat', 'lon'), may hold values from 0 to 7, as said below
- cell_source: int32 [32, 8192], P('lat', 'lon'), may hold values from 0 to 511, as said below
- land_mask: int32 [32, 8192], P('lat', 'lon'), may hold values 0 or 1
Outputs:
- spectrum_out: bfloat16 [36, 36, 32, 8192], P(None, None, 'lat', 'lon')
The draws below stay inside these ranges and needn't reach their ends.
Inputs may be any that keep to these rules, and one draw needn't show every extreme that they name: Within each band of 4 grid rows, the pairs (block_owner, block_slot) over all its rows and tile columns are distinct, each owner's slots run from 0 to its count of blocks minus one; an owner holds between 0 and 8 blocks, and at least one owner holds exactly 8. `block_slot`: see block_owner. `cell_source`: within each tile of 4 x 128 cells, the values are a permutation of 0 to 511.
All inputs are finite; a program needn't handle non-finite values. No bound on the sum of `land_mask` on one device may be relied on, other than what follows from the above.
Results may differ from the reference program's by a relative error of at most 0.001.
The reference program's roundings to bfloat16 on the way count: a program that leaves them out, or rounds other values in their place, can miss the bound.
Values may be sent and summed in bfloat16 or wider, within the bound.
A program may use at most 128 MiB of HBM per device.

```python
import math
import jax
import jax.numpy as jnp
from jax import lax

NF = 36
ND = 36
LATC = 4
LONC = 128
TILE = 512
SLOTS = 1
CAP = 8
NY = 32
NX = 8192
PTS = 262144
N_LON = 64
N_LAT = 8


def owner_layout(key):

    def group(index):
        sub = jax.random.fold_in(key, index)
        first_key, second_key, third_key = jax.random.split(sub, 3)
        half = N_LON // 2
        extra = jax.random.randint(first_key, (half,), 0, LATC + 1)
        extra = extra.at[0].set(LATC)
        counts = jnp.stack([LATC + extra, LATC - extra], axis=1).reshape(-1)
        counts = counts[jax.random.permutation(second_key, N_LON)]
        ends = jnp.cumsum(counts)
        starts = ends - counts
        blocks = jnp.arange(LATC * N_LON).astype(jnp.int32)
        owner = jnp.searchsorted(ends, blocks, side='right').astype(jnp.int32)
        slot = (blocks - starts[owner]).astype(jnp.int32)
        shuffle = jax.random.permutation(third_key, LATC * N_LON)
        return (owner[shuffle].reshape(LATC, N_LON), slot[shuffle].reshape(LATC, N_LON))
    owners, slots = jax.vmap(group)(jnp.arange(N_LAT).astype(jnp.int32))
    return (owners.reshape(N_LAT * LATC, N_LON), slots.reshape(N_LAT * LATC, N_LON))


def draw_block_owner(key, part):
    return owner_layout(jax.random.fold_in(key, 7))[0]


def draw_block_slot(key, part):
    return owner_layout(jax.random.fold_in(key, 7))[1]


def draw_cell_source(key, part):
    base = jax.random.fold_in(key, 13)
    tiles = jnp.arange(N_LAT * N_LON).astype(jnp.int32)
    perms = jax.vmap(lambda index: jax.random.permutation(jax.random.fold_in(base, index), TILE))(tiles)
    perms = perms.reshape(N_LAT, N_LON, LATC, LONC).transpose(0, 2, 1, 3)
    return perms.reshape(N_LAT * LATC, N_LON * LONC).astype(jnp.int32)


def place_ends(drawn, stream_key, low, top_value):
    shape = drawn.shape
    spot = [jax.random.randint(jax.random.fold_in(stream_key, axis), (), 0, shape[axis]) for axis in range(len(shape))]
    drawn = drawn.at[tuple(spot)].set(low)
    longest = shape.index(max(shape))
    spot[longest] = (spot[longest] + 1) % shape[longest]
    return drawn.at[tuple(spot)].set(top_value)


def block_scale(rng, extent, cuts, least, largest):
    level, own = 1.0, jax.random.fold_in(rng, 6)
    for position, parts in cuts:
        draws = jnp.exp(jax.random.uniform(jax.random.fold_in(own, position), (parts,), jnp.float32, least / len(cuts), largest / len(cuts)))
        level = level * jnp.repeat(draws, extent[position] // parts).reshape([-1 if axis == position else 1 for axis in range(len(extent))])
    return level


def centred(rng, extent, scale, bound, cuts=(), held_as=jnp.bfloat16):
    drawn = jax.random.normal(rng, extent, jnp.float32) * scale
    if len(cuts) > 0:
        drawn = block_scale(rng, extent, cuts, -0.22, 0.18) * drawn
    return jnp.clip(drawn, min=-bound, max=bound).astype(held_as)


def setup_inputs(seed: int = 0) -> dict:
    splits = jax.random.split(jax.random.key(seed), 9)
    return {
        "spec_pts": jnp.clip(jnp.exp(math.log(2.0) - 3.6927934 * jax.random.uniform(splits[0], (NF, ND, PTS), jnp.float32) ** block_scale(splits[0], (NF, ND, PTS), ((2, 512),), -0.2, 0.2)), 0.049804688, 2.0).astype(jnp.bfloat16),
        "wind_u": centred(splits[1], (PTS,), 8.0, 40.0, ((0, 512),), jnp.float32),
        "wind_v": centred(splits[2], (PTS,), 8.0, 40.0, ((0, 512),), jnp.float32),
        "ocean_current": jnp.clip(jax.random.uniform(splits[3], (2, N_LAT, N_LON * CAP, LONC), jnp.float32, -0.099609375, 0.099609375) * block_scale(splits[3], (2, N_LAT, N_LON * CAP, LONC), ((1, 8), (2, 64)), -0.4, 0.0), -0.099609375, 0.099609375).astype(jnp.bfloat16),
        "block_owner": draw_block_owner(jax.random.fold_in(splits[8], 71), 0),
        "block_slot": draw_block_slot(jax.random.fold_in(splits[8], 71), 0),
        "cell_source": draw_cell_source(jax.random.fold_in(splits[8], 71), 0),
        "land_mask": place_ends((jax.random.randint(splits[7], (NY, NX), 0, 5) < 4).astype(jnp.int32), jax.random.fold_in(splits[7], 1), 0, 1),
    }


fastest = 0.53
turn_scale = 2.5


def tables(freqs, dirs):
    ratio = 1.1 ** jnp.arange(freqs).astype(jnp.float32)
    group_speed = fastest / ratio
    phase_speed = 44.6 / ratio
    relative = ratio / ratio[freqs - 1]
    spacing = 2.0 * jnp.pi / dirs
    theta = (jnp.arange(dirs).astype(jnp.float32) + 0.5) * spacing
    facing = (jnp.arange(dirs).astype(jnp.float32) + 1.0) * spacing
    return group_speed, phase_speed, relative, jnp.cos(theta), jnp.sin(theta), jnp.cos(facing), jnp.sin(facing)


def grow(energy, proj, phase_val, rel_val, mean_energy):
    drive = jnp.maximum(proj / phase_val - 1.0, 0.0)
    gain = 0.5 * jnp.tanh(0.2 * drive)
    loss = 0.3 * rel_val * (mean_energy / 0.5) ** 2
    return (energy * jnp.exp(gain - loss)).astype(jnp.bfloat16)


def turning(ux, uy, vx, vy, face_cos, face_sin):
    return turn_scale * (face_sin * face_cos * (ux - vy) + face_sin * face_sin * uy - face_cos * face_cos * vx)


def refract(moved, turn):
    upper = jnp.roll(moved, -1, axis=0)
    flux = jnp.maximum(turn, 0.0) * moved + jnp.minimum(turn, 0.0) * upper
    return moved - (flux - jnp.roll(flux, 1, axis=0))


def reference(spec_pts, wind_u, wind_v, ocean_current, block_owner, block_slot, cell_source, land_mask):
    group_speed, phase_speed, relative, cosd, sind, face_cos, face_sin = tables(NF, ND)
    mean_energy = jnp.sum(spec_pts.astype(jnp.float32), axis=(0, 1)) / (NF * ND)
    proj = wind_u[None, :] * cosd[:, None] + wind_v[None, :] * sind[:, None]
    rows = jnp.arange(NY).astype(jnp.int32)[:, None]
    cols = jnp.arange(NX).astype(jnp.int32)[None, :]
    tile_flat = (rows // LATC) * N_LON + cols // LONC
    slot_rest = cell_source % SLOTS
    source = cell_source // SLOTS
    point = ((source % N_LON) * N_LAT + source // N_LON) * TILE + tile_flat * SLOTS + slot_rest
    index = block_owner * CAP + block_slot
    band = (jnp.arange(NY).astype(jnp.int32) // LATC)[:, None]
    current = ocean_current[:, band, index, :].reshape(2, NY, NX).astype(jnp.float32)
    east_u, east_v = current[0], current[1]
    sea = land_mask.astype(jnp.float32)
    zero_row = jnp.zeros((1, NX), jnp.float32)
    north = lambda a: jnp.concatenate([a[1:], zero_row], axis=0)
    south = lambda a: jnp.concatenate([zero_row, a[:-1]], axis=0)
    open_x = sea * jnp.roll(sea, -1, axis=1)
    face_u = 0.5 * (east_u + jnp.roll(east_u, -1, axis=1))
    open_y = sea * north(sea)
    face_v = 0.5 * (east_v + north(east_v))
    ux = 0.5 * (jnp.roll(east_u, -1, axis=1) - jnp.roll(east_u, 1, axis=1))
    vx = 0.5 * (jnp.roll(east_v, -1, axis=1) - jnp.roll(east_v, 1, axis=1))
    uy = 0.5 * (north(east_u) - south(east_u))
    vy = 0.5 * (north(east_v) - south(east_v))
    turn = turning(ux[None], uy[None], vx[None], vy[None], face_cos[:, None, None], face_sin[:, None, None])

    def one_freq(freq):
        sourced = grow(spec_pts[freq].astype(jnp.float32), proj, phase_speed[freq], relative[freq], mean_energy[None, :])
        energy = (sourced[:, point] * land_mask.astype(jnp.bfloat16)[None]).astype(jnp.float32)
        cx = group_speed[freq] * cosd[:, None, None] + face_u[None]
        flux_x = open_x[None] * (jnp.maximum(cx, 0.0) * energy + jnp.minimum(cx, 0.0) * jnp.roll(energy, -1, axis=2))
        div_x = flux_x - jnp.roll(flux_x, 1, axis=2)
        energy_n = jnp.concatenate([energy[:, 1:], jnp.zeros((ND, 1, NX), jnp.float32)], axis=1)
        cy = group_speed[freq] * sind[:, None, None] + face_v[None]
        flux_y = open_y[None] * (jnp.maximum(cy, 0.0) * energy + jnp.minimum(cy, 0.0) * energy_n)
        div_y = flux_y - jnp.concatenate([jnp.zeros((ND, 1, NX), jnp.float32), flux_y[:, :-1]], axis=1)
        moved = energy - div_x - div_y
        return (refract(moved, turn) * sea[None]).astype(jnp.bfloat16)

    return lax.map(one_freq, jnp.arange(NF).astype(jnp.int32))
```

```python
import functools
import math

import jax
import jax.numpy as jnp
import numpy as np
from jax import lax
from jax.experimental import pallas as pl
from jax.experimental.pallas import tpu as pltpu
from jax.sharding import PartitionSpec as P

NF, ND = 36, 36
SPEC = NF * ND
PAD = 1408
CELLS = 512
NK, NZX = 16, 32
CHUNKS = ((0, 384), (384, 384), (768, 384), (1152, 256))
SOURCE_GROUPS = ((0, 3), (3, 6), (6, 8), (8, 9))
READY_GROUPS = ((0, 2), (2, 5), (5, 8), (8, 9))
NC = len(CHUNKS)
GROUP = 4 * ND
HALF = ND // 2
MESH = pl.DeviceIdType.MESH
TURN_SCALE = 2.5
F32, BF16 = jnp.float32, jnp.bfloat16


def iota(shape, axis):
    return lax.broadcasted_iota(jnp.int32, shape, axis)


def onehot(cond):
    return jnp.where(cond, 1.0, 0.0).astype(BF16)


def dot(a, b, ca, cb):
    return lax.dot_general(a, b, (((ca,), (cb,)), ((), ())), preferred_element_type=F32)


def drain(ref, sem):
    pltpu.make_async_copy(ref, ref, sem).wait()


def kernel(
    spec_ref, wind_ref, dirs_ref, fscale_ref, cg_ref, cur_ref, owner_ref, slot_ref, source_ref, mask_ref,
    out_ref,
    s_ref, e_ref, hp_ref, o_ref, x1, y1, y2, z, ns_out, ns_in, ew_out, ew_in, cur_all, aux_out, aux_in,
    face_x, face_y, turn_ref, sea_ref, pick_ref,
    p1_send, p1_recv, p2_send, p2_recv, h_send, h_recv, c_sem, a_send, a_recv,
):
    lon, lat = lax.axis_index("lon"), lax.axis_index("lat")
    n_lon, n_lat = NZX * 2, NK // 2
    zx, core = lon // 2, lon % 2
    me = lat * 2 + core
    north, south = (lat + 1) % n_lat, (lat + n_lat - 1) % n_lat
    east, west = (lon + 1) % n_lon, (lon + n_lon - 1) % n_lon
    sides = ((lon, north), (lon, south), (east, lat), (west, lat))

    def dev(lo, la):
        return {"lon": lo, "lat": la}

    barrier = pltpu.get_barrier_semaphore()

    def greet1(i, _):
        k = (me + i) % NK
        pl.semaphore_signal(barrier, inc=1, device_id=dev(zx * 2 + k % 2, k // 2), device_id_type=MESH)
        return 0

    def greet2(i, _):
        t = (zx + i) % NZX
        pl.semaphore_signal(barrier, inc=1, device_id=dev(t * 2 + core, lat), device_id_type=MESH)
        return 0

    lax.fori_loop(1, NK, greet1, 0)
    lax.fori_loop(1, NZX, greet2, 0)
    for lo, la in ((east, lat), (west, lat)):
        pl.semaphore_signal(barrier, inc=1, device_id=dev(lo, la), device_id_type=MESH)

    def add(f, acc):
        return acc + spec_ref[f].astype(F32)

    total = lax.fori_loop(0, NF, add, jnp.zeros((ND, CELLS), F32))
    m0 = jnp.sum(total, axis=0, keepdims=True) / SPEC
    loss0 = 0.3 * (m0 / 0.5) ** 2
    cosd = jnp.concatenate([dirs_ref[:, :128]] * 4, axis=1)
    sind = jnp.concatenate([dirs_ref[:, 128:]] * 4, axis=1)
    proj = wind_ref[0:1, :] * cosd + wind_ref[1:2, :] * sind
    s_ref[SPEC:PAD, :] = jnp.zeros((PAD - SPEC, CELLS), F32)

    row, col = iota((CELLS, CELLS), 0), iota((CELLS, CELLS), 1)
    k, t = row // NZX, row % NZX
    by_dest = onehot(col == (k // 2) * n_lon + t * 2 + k % 2)
    regroup = onehot((row // NK == col % NZX) & (row % NK == col // NZX))

    def source(g, _):
        rows = s_ref.at[pl.ds(pl.multiple_of(g * GROUP, 16), GROUP), :]
        for i in range(4):
            f = g * 4 + i
            drive = jnp.maximum(proj * fscale_ref[f] - 1.0, 0.0)
            gain = 0.5 * jnp.tanh(0.2 * drive)
            rows[ND * i : ND * (i + 1), :] = spec_ref[f].astype(F32) * jnp.exp(gain - fscale_ref[NF + f] * loss0)
        return 0

    def send1(c):
        def one(i, _):
            k = (me + i) % NK
            pltpu.make_async_remote_copy(
                src_ref=x1[c].at[k], dst_ref=y1[c].at[me], send_sem=p1_send.at[c], recv_sem=p1_recv.at[c],
                device_id=dev(zx * 2 + k % 2, k // 2), device_id_type=MESH,
            ).start()
            return 0

        lax.fori_loop(1, NK, one, 0)
        pltpu.make_async_copy(x1[c].at[me], y1[c].at[me], p1_recv.at[c]).start()

    def send2(c):
        def one(i, _):
            t = (zx + i) % NZX
            pltpu.make_async_remote_copy(
                src_ref=y2[c].at[t], dst_ref=z[c].at[zx], send_sem=p2_send.at[c], recv_sem=p2_recv.at[c],
                device_id=dev(t * 2 + core, lat), device_id_type=MESH,
            ).start()
            return 0

        lax.fori_loop(1, NZX, one, 0)
        pltpu.make_async_copy(y2[c].at[zx], z[c].at[zx], p2_recv.at[c]).start()

    for c, (at, width) in enumerate(CHUNKS):
        lax.fori_loop(*SOURCE_GROUPS[c], source, 0)
        values = s_ref[at : at + width, :].astype(BF16)
        x1[c][...] = dot(by_dest, values, 1, 1).astype(BF16).reshape(NK, NZX, width)
        if c == 0:
            pl.semaphore_wait(barrier, NK - 1 + NZX - 1 + 2)
        send1(c)
        if c == 0:
            swap = pltpu.make_async_remote_copy(
                src_ref=cur_ref, dst_ref=cur_all.at[zx, core], send_sem=c_sem.at[0], recv_sem=c_sem.at[1],
                device_id=dev(zx * 2 + 1 - core, lat), device_id_type=MESH,
            )
            swap.start()
            pltpu.make_async_copy(cur_ref, cur_all.at[zx, core], c_sem.at[1]).start()

    drain(cur_all.at[zx], c_sem.at[1])

    def share(i, _):
        t = (zx + i) % NZX
        pltpu.make_async_remote_copy(
            src_ref=cur_all.at[zx], dst_ref=cur_all.at[zx], send_sem=c_sem.at[2], recv_sem=c_sem.at[3],
            device_id=dev(t * 2 + core, lat), device_id_type=MESH,
        ).start()
        return 0

    lax.fori_loop(1, NZX, share, 0)

    q = source_ref[...]
    where = ((q % n_lon) // 2) * NK + (q // n_lon) * 2 + q % 2
    where = jnp.where(mask_ref[...] > 0, where, -1)
    slots = iota((CELLS, 128), 0)
    for y in range(4):
        pick_ref[:, 128 * y : 128 * (y + 1)] = onehot(slots == where[y : y + 1, :])
    both = jnp.concatenate([where, where, jnp.full((8, 128), -1, jnp.int32)], axis=0)
    edge_row = iota((16, 1), 0)
    edge = jnp.where(edge_row < 4, both[:, 127:128], both[:, 0:1])
    edge_pick = onehot(iota((16, CELLS), 1) == edge)
    pr, pc = iota((32, CELLS), 0), iota((32, CELLS), 1)
    place = onehot(((pr < 4) & (pc == pr * 128)) | ((pr >= 20) & (pr < 24) & (pc == (pr - 20) * 128 + 127)))

    def halo_copies(c):
        ew = (ew_out[c], ew_in[c])
        ns = (ns_out[c], ns_in[c])
        parts = (
            (ns[0].at[1], ns[1].at[1]),
            (ns[0].at[0], ns[1].at[0]),
            (ew[0], ew[1].at[0]),
            (ew[0], ew[1].at[1]),
        )
        return [
            pltpu.make_async_remote_copy(
                src_ref=src, dst_ref=dst, send_sem=h_send.at[c, d], recv_sem=h_recv.at[c, d],
                device_id=dev(*sides[d]), device_id_type=MESH,
            )
            for d, (src, dst) in enumerate(parts)
        ]

    def aux_copies():
        return [
            pltpu.make_async_remote_copy(
                src_ref=aux_out, dst_ref=aux_in.at[d], send_sem=a_send.at[d], recv_sem=a_recv.at[d],
                device_id=dev(*sides[d]), device_id_type=MESH,
            )
            for d in range(4)
        ]

    def pick(c):
        at, width = CHUNKS[c]
        drain(z[c], p2_recv.at[c])
        got = z[c][...].reshape(CELLS, width)
        ew_out[c][...] = dot(edge_pick, got, 1, 0).astype(BF16)
        energy = dot(got, pick_ref[...], 0, 0)
        for y in range(4):
            e_ref[1 + y, at : at + width, :] = energy[:, 128 * y : 128 * (y + 1)]
        ns_out[c][0] = energy[:, :128].astype(BF16)
        ns_out[c][1] = energy[:, 384:].astype(BF16)
        for copy in halo_copies(c):
            copy.start()

    def send_aux():
        drain(cur_all.at[pl.ds(0, NZX - 1)], c_sem.at[3])
        wanted = owner_ref[...] * 16 + slot_ref[...]
        wanted = jnp.concatenate([wanted, wanted + 8, jnp.full((8, 1), -1, jnp.int32)], axis=0)
        blocks = onehot(iota((16, NZX * 32), 1) == wanted)
        found = dot(blocks, cur_all[...].reshape(NZX * 32, 128), 1, 0)
        sea = jnp.concatenate([jnp.zeros((8, 128), F32), mask_ref[...].astype(F32), jnp.zeros((4, 128), F32)], axis=0)
        aux_out[...] = (found + sea).astype(BF16)
        for copy in aux_copies():
            copy.start()

    def prepare():
        for copy in aux_copies():
            copy.wait_recv()
        own = aux_out[...].astype(F32)
        to_south, to_north, to_west, to_east = [aux_in[d].astype(F32) for d in range(4)]
        to_north = to_north * jnp.where(lat < n_lat - 1, 1.0, 0.0)
        to_south = to_south * jnp.where(lat > 0, 1.0, 0.0)
        lane = iota((16, 128), 1)
        right = jnp.where(lane == 127, pltpu.roll(to_east, 127, 1), pltpu.roll(own, 127, 1))
        left = jnp.where(lane == 0, pltpu.roll(to_west, 1, 1), pltpu.roll(own, 1, 1))
        u, v, m = own[0:4], own[4:8], own[8:12]
        ur, vr, mr = right[0:4], right[4:8], right[8:12]
        ul, vl, ml = left[0:4], left[4:8], left[8:12]
        ut = jnp.concatenate([to_south[3:4], u, to_north[0:1]], axis=0)
        vt = jnp.concatenate([to_south[7:8], v, to_north[4:5]], axis=0)
        mt = jnp.concatenate([to_south[11:12], m, to_north[8:9]], axis=0)
        fur, ful = 0.5 * (u + ur), 0.5 * (ul + u)
        oxr, oxl = m * mr, ml * m
        fv, oy = 0.5 * (vt[0:5] + vt[1:6]), mt[0:5] * mt[1:6]
        ux, vx = 0.5 * (ur - ul), 0.5 * (vr - vl)
        uy, vy = 0.5 * (ut[2:6] - ut[0:4]), 0.5 * (vt[2:6] - vt[0:4])
        wide = lambda a: jnp.broadcast_to(a, (8, 128))
        for y in range(4):
            for n, a in enumerate((fur, oxr, ful, oxl)):
                face_x[y, n] = wide(a[y : y + 1])
            sea_ref[y] = wide(m[y : y + 1])
        for y in range(5):
            face_y[y, 0] = wide(fv[y : y + 1])
            face_y[y, 1] = wide(oy[y : y + 1])
        for d in range(HALF):
            phi = (d + 1) * 2.0 * math.pi / ND
            fs, fc = math.sin(phi), math.cos(phi)
            turn = TURN_SCALE * ((fs * fc) * (ux - vy) + (fs * fs) * uy - (fc * fc) * vx)
            for y in range(4):
                turn_ref[y, d] = wide(turn[y : y + 1])

    def arrive(c):
        at, width = CHUNKS[c]
        for copy in halo_copies(c):
            copy.wait_recv()
        e_ref[0, at : at + width, :] = ns_in[c][1].astype(F32)
        e_ref[5, at : at + width, :] = ns_in[c][0].astype(F32)
        placed = dot(ew_in[c][...].reshape(32, width), place, 0, 0)
        for y in range(4):
            hp_ref[y, at : at + width, :] = placed[:, 128 * y : 128 * (y + 1)]

    lane = iota((8, 128), 1)

    def advance(step, _):
        g, y = step // 4, step % 4
        base = g * GROUP
        cg = cg_ref[g]
        fur, oxr, ful, oxl = [face_x[y, n] for n in range(4)]
        fvs, oys, fvn, oyn = face_y[y, 0], face_y[y, 1], face_y[y + 1, 0], face_y[y + 1, 1]
        sea = sea_ref[y]

        def flux(speed, here, there, is_open):
            return is_open * (speed * jnp.where(speed > 0.0, here, there))

        moved = []
        for d in range(HALF):
            theta = (d + 0.5) * 2.0 * math.pi / ND
            rows = pl.ds(base + d, 8, stride=HALF)
            here, up, down = e_ref[y + 1, rows, :], e_ref[y + 2, rows, :], e_ref[y, rows, :]
            halo = hp_ref[y, rows, :]
            right = jnp.where(lane == 127, halo, pltpu.roll(here, 127, 1))
            left = jnp.where(lane == 0, halo, pltpu.roll(here, 1, 1))
            sx, sy = cg * math.cos(theta), cg * math.sin(theta)
            div_x = flux(sx + fur, here, right, oxr) - flux(sx + ful, left, here, oxl)
            div_y = flux(sy + fvn, here, up, oyn) - flux(sy + fvs, down, here, oys)
            moved.append(here - div_x - div_y)
        half = iota((8, 128), 0) % 2
        swap = lambda a: jnp.where(half == 0, pltpu.roll(a, 7, 0), pltpu.roll(a, 1, 0))
        first = swap(moved[0])
        bent = []
        for d in range(HALF):
            turn = turn_ref[y, d]
            bent.append(turn * jnp.where(turn > 0.0, moved[d], moved[d + 1] if d + 1 < HALF else first))
        before = swap(bent[-1])
        for d in range(HALF):
            value = (moved[d] - (bent[d] - before)) * sea
            o_ref[pl.ds(g * (4 * GROUP) + d * 4 + y, 8, stride=4 * HALF), :] = value
            before = bent[d]
        return 0

    def finish(g, _):
        rows = pl.ds(pl.multiple_of(g * 4 * GROUP, 16), 4 * GROUP)
        out_ref[rows, :] = o_ref[rows, :].astype(BF16)
        return 0

    def propagate(c):
        first, last = READY_GROUPS[c]
        arrive(c)
        lax.fori_loop(first * 4, last * 4, advance, 0)
        lax.fori_loop(first, last, finish, 0)

    for c, (at, width) in enumerate(CHUNKS):
        drain(y1[c], p1_recv.at[c])
        y2[c][...] = dot(regroup, y1[c][...].reshape(CELLS, width), 1, 0).astype(BF16).reshape(NZX, NK, width)
        send2(c)
        if c == 0:
            send_aux()
        if c == 1:
            prepare()
        if c >= 1:
            pick(c - 1)
        if c >= 2:
            propagate(c - 2)
    pick(NC - 1)
    propagate(NC - 2)
    propagate(NC - 1)

    for c in range(NC):
        drain(x1[c].at[pl.ds(0, NK - 1)], p1_send.at[c])
        drain(y2[c].at[pl.ds(0, NZX - 1)], p2_send.at[c])
        for copy in halo_copies(c):
            copy.wait_send()
    drain(cur_ref, c_sem.at[0])
    drain(cur_all.at[pl.ds(0, NZX - 1)], c_sem.at[2])
    for copy in aux_copies():
        copy.wait_send()


def tables():
    ratio = 1.1 ** np.arange(NF)
    theta = (np.arange(ND) + 0.5) * 2.0 * np.pi / ND
    dirs = np.repeat(np.stack([np.cos(theta), np.sin(theta)], axis=1), 128, axis=1)
    fscale = np.concatenate([ratio / 44.6, ratio / ratio[-1]])
    speed = (0.53 / ratio).reshape(9, 4, 1) * np.array([1.0, -1.0]).reshape(1, 1, 2)
    cg = np.repeat(speed.reshape(9, 8, 1), 128, axis=2)
    return [np.asarray(a, np.float32) for a in (dirs, fscale, cg)]


def body(spec_pts, wind_u, wind_v, ocean_current, block_owner, block_slot, cell_source, land_mask):
    vmem, smem = pl.BlockSpec(memory_space=pltpu.VMEM), pl.BlockSpec(memory_space=pltpu.SMEM)
    dirs, fscale, cg = tables()
    wind = jnp.stack([wind_u, wind_v])
    per_chunk = lambda shape: [pltpu.VMEM(shape(w), BF16) for _, w in CHUNKS]
    dma = pltpu.SemaphoreType.DMA
    out = pl.pallas_call(
        kernel,
        out_shape=jax.ShapeDtypeStruct((SPEC * 4, 128), BF16),
        in_specs=[vmem, vmem, vmem, smem, vmem, vmem, vmem, vmem, vmem, vmem],
        out_specs=vmem,
        scratch_shapes=[
            pltpu.VMEM((PAD, CELLS), F32),
            pltpu.VMEM((6, PAD, 128), F32),
            pltpu.VMEM((4, PAD, 128), F32),
            pltpu.VMEM((SPEC * 4, 128), F32),
            per_chunk(lambda w: (NK, NZX, w)),
            per_chunk(lambda w: (NK, NZX, w)),
            per_chunk(lambda w: (NZX, NK, w)),
            per_chunk(lambda w: (NZX, NK, w)),
            per_chunk(lambda w: (2, w, 128)),
            per_chunk(lambda w: (2, w, 128)),
            per_chunk(lambda w: (16, w)),
            per_chunk(lambda w: (2, 16, w)),
            pltpu.VMEM((NZX, 2, 16, 128), BF16),
            pltpu.VMEM((16, 128), BF16),
            pltpu.VMEM((4, 16, 128), BF16),
            pltpu.VMEM((4, 4, 8, 128), F32),
            pltpu.VMEM((5, 2, 8, 128), F32),
            pltpu.VMEM((4, HALF, 8, 128), F32),
            pltpu.VMEM((4, 8, 128), F32),
            pltpu.VMEM((CELLS, CELLS), BF16),
            dma((NC,)), dma((NC,)), dma((NC,)), dma((NC,)), dma((NC, 4)), dma((NC, 4)), dma((4,)), dma((4,)), dma((4,)),
        ],
        compiler_params=pltpu.CompilerParams(
            collective_id=0, has_side_effects=True, vmem_limit_bytes=48 * 2**20
        ),
    )(
        spec_pts, wind, jnp.asarray(dirs), jnp.asarray(fscale), jnp.asarray(cg),
        ocean_current.reshape(16, 128), block_owner, block_slot, cell_source, land_mask,
    )
    return out.reshape(NF, ND, 4, 128)


def solution(mesh):
    return jax.shard_map(
        body,
        mesh=mesh,
        in_specs=(
            P(None, None, ("lon", "lat")),
            P(("lon", "lat")),
            P(("lon", "lat")),
            P(None, "lat", "lon", None),
            P("lat", "lon"),
            P("lat", "lon"),
            P("lat", "lon"),
            P("lat", "lon"),
        ),
        out_specs=P(None, None, "lat", "lon"),
        check_vma=False,
    )
```

```python
import functools
import math

import jax
import jax.numpy as jnp
import numpy as np
from jax import lax
from jax.experimental import pallas as pl
from jax.experimental.pallas import tpu as pltpu
from jax.sharding import PartitionSpec as P

NF, ND = 36, 36
SPEC = NF * ND
PAD = 1408
CELLS = 512
NK, NZX = 16, 32
WIDTHS = (512, 128, 640, 128)
FIRST = (0, 0, 1, 1)
CHUNKS = tuple((sum(WIDTHS[:i]), w) for i, w in enumerate(WIDTHS))
SHAPES = ((NK, NZX), (NZX, NK))
HELD = tuple(min(w, SPEC - at) for at, w in CHUNKS)
NC = len(CHUNKS)
LOADS = 4
GROUP = 4 * ND


def spans(counts):
    return tuple(zip((0,) + counts[:-1], counts))


READY_GROUPS = spans(tuple(min((at + w) // GROUP, SPEC // GROUP) for at, w in CHUNKS))
HALF = ND // 2
MESH = pl.DeviceIdType.MESH
TURN_SCALE = 2.5
F32, BF16 = jnp.float32, jnp.bfloat16


def iota(shape, axis):
    return lax.broadcasted_iota(jnp.int32, shape, axis)


def onehot(cond):
    return jnp.where(cond, 1.0, 0.0).astype(BF16)


def dot(a, b, ca, cb):
    return lax.dot_general(a, b, (((ca,), (cb,)), ((), ())), preferred_element_type=F32)


def drain(ref, sem):
    pltpu.make_async_copy(ref, ref, sem).wait()


def kernel(
    spec_hbm, wu_hbm, wv_hbm, table_hbm, cur_ref, owner_hbm, slot_hbm, source_hbm, mask_hbm,
    out_hbm,
    out_ref, spec_ref, wu_ref, wv_ref, table_ref, owner_ref, slot_ref, source_ref, mask_ref,
    s_ref, e_ref, hp_ref, o_ref, x1, y1, y2, z, ns_out, ns_in, ew_out, ew_in, cur_all, aux_out, aux_in,
    face_x, face_y, turn_ref, sea_ref, pick_ref,
    p1_send, p1_recv, p2_send, p2_recv, h_send, h_recv, c_sem, a_send, a_recv, in_sem, out_sem,
):
    lon, lat = lax.axis_index("lon"), lax.axis_index("lat")
    n_lon, n_lat = NZX * 2, NK // 2
    zx, core = lon // 2, lon % 2
    me = lat * 2 + core
    north, south = (lat + 1) % n_lat, (lat + n_lat - 1) % n_lat
    east, west = (lon + 1) % n_lon, (lon + n_lon - 1) % n_lon
    sides = ((lon, north), (lon, south), (east, lat), (west, lat))

    def dev(lo, la):
        return {"lon": lo, "lat": la}

    small = (
        (wu_hbm, wu_ref), (wv_hbm, wv_ref), (table_hbm, table_ref), (owner_hbm, owner_ref), (slot_hbm, slot_ref),
        (source_hbm, source_ref), (mask_hbm, mask_ref),
    )
    parts = [pl.ds(i * (NF // LOADS), NF // LOADS) for i in range(LOADS)]
    loads = [pltpu.make_async_copy(spec_hbm.at[p], spec_ref.at[p], in_sem.at[i]) for i, p in enumerate(parts)]
    loads += [pltpu.make_async_copy(a, b, in_sem.at[LOADS + i]) for i, (a, b) in enumerate(small)]
    for load in loads:
        load.start()
    barrier = pltpu.get_barrier_semaphore()

    def greet1(i, _):
        k = (me + i) % NK
        pl.semaphore_signal(barrier, inc=1, device_id=dev(zx * 2 + k % 2, k // 2), device_id_type=MESH)
        return 0

    def greet2(i, _):
        t = (zx + i) % NZX
        pl.semaphore_signal(barrier, inc=1, device_id=dev(t * 2 + core, lat), device_id_type=MESH)
        return 0

    lax.fori_loop(1, NK, greet1, 0)
    lax.fori_loop(1, NZX, greet2, 0)
    for lo, la in ((east, lat), (west, lat)):
        pl.semaphore_signal(barrier, inc=1, device_id=dev(lo, la), device_id_type=MESH)

    def add(f, acc):
        return acc + spec_ref[f].astype(F32)

    total = jnp.zeros((ND, CELLS), F32)
    for i in range(LOADS):
        loads[i].wait()
        total = lax.fori_loop(i * (NF // LOADS), (i + 1) * (NF // LOADS), add, total)
    for load in loads[LOADS:]:
        load.wait()
    m0 = jnp.sum(total, axis=0, keepdims=True) / SPEC
    loss0 = 0.3 * (m0 / 0.5) ** 2
    across = lambda a: jnp.concatenate([a] * 4, axis=1)
    proj = wu_ref[...] * across(table_ref[0:ND, :]) + wv_ref[...] * across(table_ref[40 : 40 + ND, :])
    s_ref[SPEC:PAD, :] = jnp.zeros((PAD - SPEC, CELLS), F32)

    row, col = iota((CELLS, CELLS), 0), iota((CELLS, CELLS), 1)
    by_dest, regroup = [], []
    for rows_of, columns_of in (SHAPES, SHAPES[::-1]):
        minor, other = rows_of[1], columns_of[1]
        major, rest = row // minor, row % minor
        k, t = (major, rest) if minor == NZX else (rest, major)
        by_dest.append(onehot(col == (k // 2) * n_lon + t * 2 + k % 2))
        regroup.append(onehot((row // other == col % minor) & (row % other == col // minor)))

    def source(g, _):
        rows = s_ref.at[pl.ds(pl.multiple_of(g * GROUP, 16), GROUP), :]
        for i in range(4):
            f = g * 4 + i
            per_speed = across(table_ref[pl.ds(152 + f, 1), :])
            rel = across(table_ref[pl.ds(192 + f, 1), :])
            drive = jnp.maximum(proj * per_speed - 1.0, 0.0)
            gain = 0.5 * jnp.tanh(0.2 * drive)
            rows[ND * i : ND * (i + 1), :] = spec_ref[f].astype(F32) * jnp.exp(gain - rel * loss0)
        return 0

    def exchange(axis, src, dst, send, recv):
        n, mine = ((NK, me), (NZX, zx))[axis]

        def one(i, _):
            to = (mine + i) % n
            pltpu.make_async_remote_copy(
                src_ref=src.at[to], dst_ref=dst.at[mine], send_sem=send, recv_sem=recv,
                device_id=(dev(zx * 2 + to % 2, to // 2), dev(to * 2 + core, lat))[axis], device_id_type=MESH,
            ).start()
            return 0

        lax.fori_loop(1, n, one, 0)
        pltpu.make_async_copy(src.at[mine], dst.at[mine], recv).start()

    def send1(c):
        exchange(FIRST[c], x1[c], y1[c], p1_send.at[c], p1_recv.at[c])

    def send2(c):
        exchange(1 - FIRST[c], y2[c], z[c], p2_send.at[c], p2_recv.at[c])

    def dispatch(c):
        at, width = CHUNKS[c]
        values = s_ref[at : at + width, :].astype(BF16)
        x1[c][...] = dot(by_dest[FIRST[c]], values, 1, 1).astype(BF16).reshape(*SHAPES[FIRST[c]], width)

    def middle(c):
        width = CHUNKS[c][1]
        drain(y1[c], p1_recv.at[c])
        values = dot(regroup[FIRST[c]], y1[c][...].reshape(CELLS, width), 1, 0)
        y2[c][...] = values.astype(BF16).reshape(*SHAPES[1 - FIRST[c]], width)
        send2(c)

    def share(i, _):
        t = (zx + i) % NZX
        pltpu.make_async_remote_copy(
            src_ref=cur_ref, dst_ref=cur_all.at[core, zx], send_sem=c_sem.at[0], recv_sem=c_sem.at[1],
            device_id=dev(t * 2 + core, lat), device_id_type=MESH,
        ).start()
        return 0

    swap = pltpu.make_async_remote_copy(
        src_ref=cur_all.at[core], dst_ref=cur_all.at[core], send_sem=c_sem.at[2], recv_sem=c_sem.at[3],
        device_id=dev(zx * 2 + 1 - core, lat), device_id_type=MESH,
    )

    first_groups = -(-WIDTHS[0] // GROUP)
    lax.fori_loop(0, first_groups, source, 0)
    dispatch(0)
    pl.semaphore_wait(barrier, NK - 1 + NZX - 1 + 2)
    send1(0)
    lax.fori_loop(first_groups, SPEC // GROUP, source, 0)
    dispatch(2)
    send1(2)
    lax.fori_loop(1, NZX, share, 0)
    pltpu.make_async_copy(cur_ref, cur_all.at[core, zx], c_sem.at[1]).start()
    dispatch(1)
    dispatch(3)

    q = source_ref[...]
    from_k, from_t = (q // n_lon) * 2 + q % 2, (q % n_lon) // 2
    slots = iota((CELLS, 128), 0)
    edge_row = iota((16, 1), 0)
    edge_pick = []
    for kind, where in enumerate((from_t * NK + from_k, from_k * NZX + from_t)):
        where = jnp.where(mask_ref[...] > 0, where, -1)
        for y in range(4):
            pick_ref[kind, :, 128 * y : 128 * (y + 1)] = onehot(slots == where[y : y + 1, :])
        both = jnp.concatenate([where, where, jnp.full((8, 128), -1, jnp.int32)], axis=0)
        edge = jnp.where(edge_row < 4, both[:, 127:128], both[:, 0:1])
        edge_pick.append(onehot(iota((16, CELLS), 1) == edge))
    pr, pc = iota((32, CELLS), 0), iota((32, CELLS), 1)
    place = onehot(((pr < 4) & (pc == pr * 128)) | ((pr >= 20) & (pr < 24) & (pc == (pr - 20) * 128 + 127)))

    def halo_copies(c):
        ew = (ew_out[c], ew_in[c])
        ns = (ns_out[c], ns_in[c])
        parts = (
            (ns[0].at[1], ns[1].at[1]),
            (ns[0].at[0], ns[1].at[0]),
            (ew[0], ew[1].at[0]),
            (ew[0], ew[1].at[1]),
        )
        return [
            pltpu.make_async_remote_copy(
                src_ref=src, dst_ref=dst, send_sem=h_send.at[c, d], recv_sem=h_recv.at[c, d],
                device_id=dev(*sides[d]), device_id_type=MESH,
            )
            for d, (src, dst) in enumerate(parts)
        ]

    def aux_copies():
        return [
            pltpu.make_async_remote_copy(
                src_ref=aux_out, dst_ref=aux_in.at[d], send_sem=a_send.at[d], recv_sem=a_recv.at[d],
                device_id=dev(*sides[d]), device_id_type=MESH,
            )
            for d in range(4)
        ]

    def pick(c):
        at, width = CHUNKS[c]
        drain(z[c], p2_recv.at[c])
        got = z[c][...].reshape(CELLS, width)
        ew_out[c][...] = dot(edge_pick[FIRST[c]], got, 1, 0).astype(BF16)
        energy = dot(got, pick_ref[FIRST[c]], 0, 0)
        for y in range(4):
            e_ref[1 + y, at : at + width, :] = energy[:, 128 * y : 128 * (y + 1)]
        ns_out[c][0] = energy[: HELD[c], :128].astype(BF16)
        ns_out[c][1] = energy[: HELD[c], 384:].astype(BF16)
        for copy in halo_copies(c):
            copy.start()

    def send_aux():
        swap.wait_recv()
        owner = owner_ref[...]
        wanted = ((owner % 2) * NZX + owner // 2) * 16 + slot_ref[...]
        r, n = iota((16, 4), 0), iota((16, 4), 1)
        wanted = jnp.where(r % 4 == n, wanted + 8 * (r // 4), 0).astype(F32)
        wanted = jnp.sum(wanted, axis=1, keepdims=True).astype(jnp.int32)
        wanted = jnp.where(iota((16, 1), 0) < 8, wanted, -1)
        blocks = onehot(iota((16, NZX * 32), 1) == wanted)
        found = dot(blocks, cur_all[...].reshape(NZX * 32, 128), 1, 0)
        sea = jnp.concatenate([jnp.zeros((8, 128), F32), mask_ref[...].astype(F32), jnp.zeros((4, 128), F32)], axis=0)
        aux_out[...] = (found + sea).astype(BF16)
        for copy in aux_copies():
            copy.start()

    def prepare():
        for copy in aux_copies():
            copy.wait_recv()
        own = aux_out[...].astype(F32)
        to_south, to_north, to_west, to_east = [aux_in[d].astype(F32) for d in range(4)]
        to_north = to_north * jnp.where(lat < n_lat - 1, 1.0, 0.0)
        to_south = to_south * jnp.where(lat > 0, 1.0, 0.0)
        lane = iota((16, 128), 1)
        right = jnp.where(lane == 127, pltpu.roll(to_east, 127, 1), pltpu.roll(own, 127, 1))
        left = jnp.where(lane == 0, pltpu.roll(to_west, 1, 1), pltpu.roll(own, 1, 1))
        u, v, m = own[0:4], own[4:8], own[8:12]
        ur, vr, mr = right[0:4], right[4:8], right[8:12]
        ul, vl, ml = left[0:4], left[4:8], left[8:12]
        ut = jnp.concatenate([to_south[3:4], u, to_north[0:1]], axis=0)
        vt = jnp.concatenate([to_south[7:8], v, to_north[4:5]], axis=0)
        mt = jnp.concatenate([to_south[11:12], m, to_north[8:9]], axis=0)
        fur, ful = 0.5 * (u + ur), 0.5 * (ul + u)
        oxr, oxl = m * mr, ml * m
        fv, oy = 0.5 * (vt[0:5] + vt[1:6]), mt[0:5] * mt[1:6]
        ux, vx = 0.5 * (ur - ul), 0.5 * (vr - vl)
        uy, vy = 0.5 * (ut[2:6] - ut[0:4]), 0.5 * (vt[2:6] - vt[0:4])
        wide = lambda a: jnp.broadcast_to(a, (8, 128))
        for y in range(4):
            for n, a in enumerate((fur, oxr, ful, oxl)):
                face_x[y, n] = wide(a[y : y + 1])
            sea_ref[y] = wide(m[y : y + 1])
        for y in range(5):
            face_y[y, 0] = wide(fv[y : y + 1])
            face_y[y, 1] = wide(oy[y : y + 1])
        for d in range(HALF):
            phi = (d + 1) * 2.0 * math.pi / ND
            fs, fc = math.sin(phi), math.cos(phi)
            turn = TURN_SCALE * ((fs * fc) * (ux - vy) + (fs * fs) * uy - (fc * fc) * vx)
            for y in range(4):
                turn_ref[y, d] = wide(turn[y : y + 1])

    def arrive(c):
        at, width = CHUNKS[c]
        for copy in halo_copies(c):
            copy.wait_recv()
        e_ref[0, at : at + HELD[c], :] = ns_in[c][1].astype(F32)
        e_ref[5, at : at + HELD[c], :] = ns_in[c][0].astype(F32)
        placed = dot(ew_in[c][...].reshape(32, width), place, 0, 0)
        for y in range(4):
            hp_ref[y, at : at + width, :] = placed[:, 128 * y : 128 * (y + 1)]

    lane = iota((8, 128), 1)

    def advance(step, _):
        g, y = step // 4, step % 4
        base = g * GROUP
        cg = table_ref[pl.ds(pl.multiple_of(80 + g * 8, 8), 8), :]
        fur, oxr, ful, oxl = [face_x[y, n] for n in range(4)]
        fvs, oys, fvn, oyn = face_y[y, 0], face_y[y, 1], face_y[y + 1, 0], face_y[y + 1, 1]
        sea = sea_ref[y]

        def flux(speed, here, there, is_open):
            return is_open * (speed * jnp.where(speed > 0.0, here, there))

        moved = []
        for d in range(HALF):
            theta = (d + 0.5) * 2.0 * math.pi / ND
            rows = pl.ds(base + d, 8, stride=HALF)
            here, up, down = e_ref[y + 1, rows, :], e_ref[y + 2, rows, :], e_ref[y, rows, :]
            halo = hp_ref[y, rows, :]
            right = jnp.where(lane == 127, halo, pltpu.roll(here, 127, 1))
            left = jnp.where(lane == 0, halo, pltpu.roll(here, 1, 1))
            sx, sy = cg * math.cos(theta), cg * math.sin(theta)
            div_x = flux(sx + fur, here, right, oxr) - flux(sx + ful, left, here, oxl)
            div_y = flux(sy + fvn, here, up, oyn) - flux(sy + fvs, down, here, oys)
            moved.append(here - div_x - div_y)
        half = iota((8, 128), 0) % 2
        swap = lambda a: jnp.where(half == 0, pltpu.roll(a, 7, 0), pltpu.roll(a, 1, 0))
        first = swap(moved[0])
        bent = []
        for d in range(HALF):
            turn = turn_ref[y, d]
            bent.append(turn * jnp.where(turn > 0.0, moved[d], moved[d + 1] if d + 1 < HALF else first))
        before = swap(bent[-1])
        for d in range(HALF):
            value = (moved[d] - (bent[d] - before)) * sea
            o_ref[pl.ds(g * (4 * GROUP) + d * 4 + y, 8, stride=4 * HALF), :] = value
            before = bent[d]
        return 0

    def finish(g, _):
        rows = pl.ds(pl.multiple_of(g * 4 * GROUP, 16), 4 * GROUP)
        out_ref[rows, :] = o_ref[rows, :].astype(BF16)
        pltpu.make_async_copy(out_ref.at[rows, :], out_hbm.at[rows, :], out_sem).start()
        return 0

    def propagate(c):
        first, last = READY_GROUPS[c]
        arrive(c)
        lax.fori_loop(first * 4, last * 4, advance, 0)
        lax.fori_loop(first, last, finish, 0)

    middle(0)
    send1(1)
    drain(cur_all.at[core], c_sem.at[1])
    swap.start()
    middle(2)
    send1(3)
    send_aux()
    middle(1)
    middle(3)
    prepare()
    pick(0)
    pick(1)
    propagate(0)
    pick(2)
    propagate(1)
    pick(3)
    propagate(2)
    propagate(3)

    for c in range(NC):
        drain(x1[c].at[pl.ds(0, SHAPES[FIRST[c]][0] - 1)], p1_send.at[c])
        drain(y2[c].at[pl.ds(0, SHAPES[1 - FIRST[c]][0] - 1)], p2_send.at[c])
        for copy in halo_copies(c):
            copy.wait_send()
    drain(cur_all.at[core, pl.ds(0, NZX - 1)], c_sem.at[0])
    swap.wait_send()
    for copy in aux_copies():
        copy.wait_send()
    drain(out_ref, out_sem)


def tables():
    ratio = 1.1 ** np.arange(NF)
    theta = (np.arange(ND) + 0.5) * 2.0 * np.pi / ND
    table = np.zeros((232, 1))
    table[0:ND, 0] = np.cos(theta)
    table[40 : 40 + ND, 0] = np.sin(theta)
    table[80:152, 0] = np.repeat(0.53 / ratio, 2) * np.tile([1.0, -1.0], NF)
    table[152 : 152 + NF, 0] = ratio / 44.6
    table[192 : 192 + NF, 0] = ratio / ratio[-1]
    return np.repeat(table, 128, axis=1).astype(np.float32)


def body(spec_pts, wind_u, wind_v, ocean_current, block_owner, block_slot, cell_source, land_mask):
    hbm = pl.BlockSpec(memory_space=pltpu.HBM)
    per_chunk = lambda shape: [pltpu.VMEM(shape(i, w), BF16) for i, w in enumerate(WIDTHS)]
    dma = pltpu.SemaphoreType.DMA
    out = pl.pallas_call(
        kernel,
        out_shape=jax.ShapeDtypeStruct((SPEC * 4, 128), BF16),
        in_specs=[hbm] * 9,
        out_specs=hbm,
        scratch_shapes=[
            pltpu.VMEM((SPEC * 4, 128), BF16),
            pltpu.VMEM((NF, ND, CELLS), BF16),
            pltpu.VMEM((1, CELLS), F32),
            pltpu.VMEM((1, CELLS), F32),
            pltpu.VMEM((232, 128), F32),
            pltpu.VMEM((1, 4), jnp.int32),
            pltpu.VMEM((1, 4), jnp.int32),
            pltpu.VMEM((4, 128), jnp.int32),
            pltpu.VMEM((4, 128), jnp.int32),
            pltpu.VMEM((PAD, CELLS), F32),
            pltpu.VMEM((6, PAD, 128), F32),
            pltpu.VMEM((4, PAD, 128), F32),
            pltpu.VMEM((SPEC * 4, 128), F32),
            per_chunk(lambda i, w: (*SHAPES[FIRST[i]], w)),
            per_chunk(lambda i, w: (*SHAPES[FIRST[i]], w)),
            per_chunk(lambda i, w: (*SHAPES[1 - FIRST[i]], w)),
            per_chunk(lambda i, w: (*SHAPES[1 - FIRST[i]], w)),
            per_chunk(lambda i, w: (2, HELD[i], 128)),
            per_chunk(lambda i, w: (2, HELD[i], 128)),
            per_chunk(lambda i, w: (16, w)),
            per_chunk(lambda i, w: (2, 16, w)),
            pltpu.VMEM((2, NZX, 16, 128), BF16),
            pltpu.VMEM((16, 128), BF16),
            pltpu.VMEM((4, 16, 128), BF16),
            pltpu.VMEM((4, 4, 8, 128), F32),
            pltpu.VMEM((5, 2, 8, 128), F32),
            pltpu.VMEM((4, HALF, 8, 128), F32),
            pltpu.VMEM((4, 8, 128), F32),
            pltpu.VMEM((2, CELLS, CELLS), BF16),
            dma((NC,)), dma((NC,)), dma((NC,)), dma((NC,)), dma((NC, 4)), dma((NC, 4)), dma((4,)), dma((4,)), dma((4,)),
            dma((LOADS + 7,)), dma(()),
        ],
        compiler_params=pltpu.CompilerParams(
            collective_id=0, has_side_effects=True, vmem_limit_bytes=60 * 2**20
        ),
    )(
        spec_pts, wind_u.reshape(1, CELLS), wind_v.reshape(1, CELLS), jnp.asarray(tables()),
        ocean_current.reshape(16, 128), block_owner.T, block_slot.T, cell_source, land_mask,
    )
    return out.reshape(NF, ND, 4, 128)


def solution(mesh):
    return jax.shard_map(
        body,
        mesh=mesh,
        in_specs=(
            P(None, None, ("lon", "lat")),
            P(("lon", "lat")),
            P(("lon", "lat")),
            P(None, "lat", "lon", None),
            P("lat", "lon"),
            P("lat", "lon"),
            P("lat", "lon"),
            P("lat", "lon"),
        ),
        out_specs=P(None, None, "lat", "lon"),
        check_vma=False,
    )
```

```python
import functools
import math

import jax
import jax.numpy as jnp
import numpy as np
from jax import lax
from jax.experimental import pallas as pl
from jax.experimental.pallas import tpu as pltpu
from jax.sharding import PartitionSpec as P

NF, ND = 36, 36
SPEC = NF * ND
PAD = 1408
CELLS = 512
NK, NZX = 16, 32
WIDTHS = (384, 384, 512, 128)
FIRST = (0, 0, 1, 1)
CHUNKS = tuple((sum(WIDTHS[:i]), w) for i, w in enumerate(WIDTHS))
SHAPES = ((NK, NZX), (NZX, NK))
HELD = tuple(min(w, SPEC - at) for at, w in CHUNKS)
NC = len(CHUNKS)
LOADS = 4
GROUP = 4 * ND


def spans(counts):
    return tuple(zip((0,) + counts[:-1], counts))


READY_GROUPS = spans(tuple(min((at + w) // GROUP, SPEC // GROUP) for at, w in CHUNKS))
HALF = ND // 2
MESH = pl.DeviceIdType.MESH
TURN_SCALE = 2.5
F32, BF16 = jnp.float32, jnp.bfloat16


def iota(shape, axis):
    return lax.broadcasted_iota(jnp.int32, shape, axis)


def onehot(cond):
    return jnp.where(cond, 1.0, 0.0).astype(BF16)


def dot(a, b, ca, cb):
    return lax.dot_general(a, b, (((ca,), (cb,)), ((), ())), preferred_element_type=F32)


def drain(ref, sem):
    pltpu.make_async_copy(ref, ref, sem).wait()


def kernel(
    spec_hbm, wu_hbm, wv_hbm, table_hbm, cur_ref, owner_hbm, slot_hbm, source_hbm, mask_hbm,
    out_ref,
    spec_ref, wu_ref, wv_ref, table_ref, owner_ref, slot_ref, source_ref, mask_ref,
    s_ref, e_ref, hp_ref, o_ref, x1, y1, y2, z, ns_out, ns_in, ew_out, ew_in, cur_all, aux_out, aux_in,
    face_x, face_y, turn_ref, sea_ref, pick_ref,
    p1_send, p1_recv, p2_send, p2_recv, h_send, h_recv, c_sem, a_send, a_recv, in_sem,
):
    lon, lat = lax.axis_index("lon"), lax.axis_index("lat")
    n_lon, n_lat = NZX * 2, NK // 2
    zx, core = lon // 2, lon % 2
    me = lat * 2 + core
    north, south = (lat + 1) % n_lat, (lat + n_lat - 1) % n_lat
    east, west = (lon + 1) % n_lon, (lon + n_lon - 1) % n_lon
    sides = ((lon, north), (lon, south), (east, lat), (west, lat))

    def dev(lo, la):
        return {"lon": lo, "lat": la}

    small = (
        (wu_hbm, wu_ref), (wv_hbm, wv_ref), (table_hbm, table_ref), (owner_hbm, owner_ref), (slot_hbm, slot_ref),
        (source_hbm, source_ref), (mask_hbm, mask_ref),
    )
    parts = [pl.ds(i * (NF // LOADS), NF // LOADS) for i in range(LOADS)]
    loads = [pltpu.make_async_copy(spec_hbm.at[p], spec_ref.at[p], in_sem.at[i]) for i, p in enumerate(parts)]
    loads += [pltpu.make_async_copy(a, b, in_sem.at[LOADS + i]) for i, (a, b) in enumerate(small)]
    for load in loads:
        load.start()
    barrier = pltpu.get_barrier_semaphore()

    def greet1(i, _):
        k = (me + i) % NK
        pl.semaphore_signal(barrier, inc=1, device_id=dev(zx * 2 + k % 2, k // 2), device_id_type=MESH)
        return 0

    def greet2(i, _):
        t = (zx + i) % NZX
        pl.semaphore_signal(barrier, inc=1, device_id=dev(t * 2 + core, lat), device_id_type=MESH)
        return 0

    lax.fori_loop(1, NK, greet1, 0)
    lax.fori_loop(1, NZX, greet2, 0)
    for lo, la in ((east, lat), (west, lat)):
        pl.semaphore_signal(barrier, inc=1, device_id=dev(lo, la), device_id_type=MESH)

    def add(f, acc):
        return acc + spec_ref[f].astype(F32)

    total = jnp.zeros((ND, CELLS), F32)
    for i in range(LOADS):
        loads[i].wait()
        total = lax.fori_loop(i * (NF // LOADS), (i + 1) * (NF // LOADS), add, total)
    for load in loads[LOADS:]:
        load.wait()
    m0 = jnp.sum(total, axis=0, keepdims=True) / SPEC
    loss0 = 0.3 * (m0 / 0.5) ** 2
    across = lambda a: jnp.concatenate([a] * 4, axis=1)
    proj = wu_ref[...] * across(table_ref[0:ND, :]) + wv_ref[...] * across(table_ref[40 : 40 + ND, :])
    s_ref[SPEC:PAD, :] = jnp.zeros((PAD - SPEC, CELLS), F32)

    row, col = iota((CELLS, CELLS), 0), iota((CELLS, CELLS), 1)
    by_dest, regroup = [], []
    for rows_of, columns_of in (SHAPES, SHAPES[::-1]):
        minor, other = rows_of[1], columns_of[1]
        major, rest = row // minor, row % minor
        k, t = (major, rest) if minor == NZX else (rest, major)
        by_dest.append(onehot(col == (k // 2) * n_lon + t * 2 + k % 2))
        regroup.append(onehot((row // other == col % minor) & (row % other == col // minor)))

    def source(g, _):
        rows = s_ref.at[pl.ds(pl.multiple_of(g * GROUP, 16), GROUP), :]
        for i in range(4):
            f = g * 4 + i
            per_speed = across(table_ref[pl.ds(152 + f, 1), :])
            rel = across(table_ref[pl.ds(192 + f, 1), :])
            drive = jnp.maximum(proj * per_speed - 1.0, 0.0)
            gain = 0.5 * jnp.tanh(0.2 * drive)
            rows[ND * i : ND * (i + 1), :] = spec_ref[f].astype(F32) * jnp.exp(gain - rel * loss0)
        return 0

    def exchange(axis, src, dst, send, recv):
        n, mine = ((NK, me), (NZX, zx))[axis]

        def one(i, _):
            to = (mine + i) % n
            pltpu.make_async_remote_copy(
                src_ref=src.at[to], dst_ref=dst.at[mine], send_sem=send, recv_sem=recv,
                device_id=(dev(zx * 2 + to % 2, to // 2), dev(to * 2 + core, lat))[axis], device_id_type=MESH,
            ).start()
            return 0

        lax.fori_loop(1, n, one, 0)
        pltpu.make_async_copy(src.at[mine], dst.at[mine], recv).start()

    def send1(c):
        exchange(FIRST[c], x1[c], y1[c], p1_send.at[c], p1_recv.at[c])

    def send2(c):
        exchange(1 - FIRST[c], y2[c], z[c], p2_send.at[c], p2_recv.at[c])

    def dispatch(c):
        at, width = CHUNKS[c]
        values = s_ref[at : at + width, :].astype(BF16)
        x1[c][...] = dot(by_dest[FIRST[c]], values, 1, 1).astype(BF16).reshape(*SHAPES[FIRST[c]], width)

    def middle(c):
        width = CHUNKS[c][1]
        drain(y1[c], p1_recv.at[c])
        values = dot(regroup[FIRST[c]], y1[c][...].reshape(CELLS, width), 1, 0)
        y2[c][...] = values.astype(BF16).reshape(*SHAPES[1 - FIRST[c]], width)
        send2(c)

    def share(i, _):
        t = (zx + i) % NZX
        pltpu.make_async_remote_copy(
            src_ref=cur_ref, dst_ref=cur_all.at[core, zx], send_sem=c_sem.at[0], recv_sem=c_sem.at[1],
            device_id=dev(t * 2 + core, lat), device_id_type=MESH,
        ).start()
        return 0

    swap = pltpu.make_async_remote_copy(
        src_ref=cur_all.at[core], dst_ref=cur_all.at[core], send_sem=c_sem.at[2], recv_sem=c_sem.at[3],
        device_id=dev(zx * 2 + 1 - core, lat), device_id_type=MESH,
    )

    first_groups = -(-WIDTHS[0] // GROUP)
    lax.fori_loop(0, first_groups, source, 0)
    dispatch(0)
    pl.semaphore_wait(barrier, NK - 1 + NZX - 1 + 2)
    send1(0)
    lax.fori_loop(first_groups, SPEC // GROUP, source, 0)
    dispatch(2)
    send1(2)
    lax.fori_loop(1, NZX, share, 0)
    pltpu.make_async_copy(cur_ref, cur_all.at[core, zx], c_sem.at[1]).start()
    dispatch(1)
    dispatch(3)

    q = source_ref[...]
    from_k, from_t = (q // n_lon) * 2 + q % 2, (q % n_lon) // 2
    slots = iota((CELLS, 128), 0)
    edge_row = iota((16, 1), 0)
    edge_pick = []
    for kind, where in enumerate((from_t * NK + from_k, from_k * NZX + from_t)):
        where = jnp.where(mask_ref[...] > 0, where, -1)
        for y in range(4):
            pick_ref[kind, :, 128 * y : 128 * (y + 1)] = onehot(slots == where[y : y + 1, :])
        both = jnp.concatenate([where, where, jnp.full((8, 128), -1, jnp.int32)], axis=0)
        edge = jnp.where(edge_row < 4, both[:, 127:128], both[:, 0:1])
        edge_pick.append(onehot(iota((16, CELLS), 1) == edge))
    pr, pc = iota((32, CELLS), 0), iota((32, CELLS), 1)
    place = onehot(((pr < 4) & (pc == pr * 128)) | ((pr >= 20) & (pr < 24) & (pc == (pr - 20) * 128 + 127)))

    def halo_copies(c):
        ew = (ew_out[c], ew_in[c])
        ns = (ns_out[c], ns_in[c])
        parts = (
            (ns[0].at[1], ns[1].at[1]),
            (ns[0].at[0], ns[1].at[0]),
            (ew[0], ew[1].at[0]),
            (ew[0], ew[1].at[1]),
        )
        return [
            pltpu.make_async_remote_copy(
                src_ref=src, dst_ref=dst, send_sem=h_send.at[c, d], recv_sem=h_recv.at[c, d],
                device_id=dev(*sides[d]), device_id_type=MESH,
            )
            for d, (src, dst) in enumerate(parts)
        ]

    def aux_copies():
        return [
            pltpu.make_async_remote_copy(
                src_ref=aux_out, dst_ref=aux_in.at[d], send_sem=a_send.at[d], recv_sem=a_recv.at[d],
                device_id=dev(*sides[d]), device_id_type=MESH,
            )
            for d in range(4)
        ]

    def pick(c):
        at, width = CHUNKS[c]
        drain(z[c], p2_recv.at[c])
        got = z[c][...].reshape(CELLS, width)
        ew_out[c][...] = dot(edge_pick[FIRST[c]], got, 1, 0).astype(BF16)
        energy = dot(got, pick_ref[FIRST[c]], 0, 0)
        for y in range(4):
            e_ref[1 + y, at : at + width, :] = energy[:, 128 * y : 128 * (y + 1)]
        ns_out[c][0] = energy[: HELD[c], :128].astype(BF16)
        ns_out[c][1] = energy[: HELD[c], 384:].astype(BF16)
        for copy in halo_copies(c):
            copy.start()

    def send_aux():
        swap.wait_recv()
        owner = owner_ref[...]
        wanted = ((owner % 2) * NZX + owner // 2) * 16 + slot_ref[...]
        r, n = iota((16, 4), 0), iota((16, 4), 1)
        wanted = jnp.where(r % 4 == n, wanted + 8 * (r // 4), 0).astype(F32)
        wanted = jnp.sum(wanted, axis=1, keepdims=True).astype(jnp.int32)
        wanted = jnp.where(iota((16, 1), 0) < 8, wanted, -1)
        blocks = onehot(iota((16, NZX * 32), 1) == wanted)
        found = dot(blocks, cur_all[...].reshape(NZX * 32, 128), 1, 0)
        sea = jnp.concatenate([jnp.zeros((8, 128), F32), mask_ref[...].astype(F32), jnp.zeros((4, 128), F32)], axis=0)
        aux_out[...] = (found + sea).astype(BF16)
        for copy in aux_copies():
            copy.start()

    def prepare():
        for copy in aux_copies():
            copy.wait_recv()
        own = aux_out[...].astype(F32)
        to_south, to_north, to_west, to_east = [aux_in[d].astype(F32) for d in range(4)]
        to_north = to_north * jnp.where(lat < n_lat - 1, 1.0, 0.0)
        to_south = to_south * jnp.where(lat > 0, 1.0, 0.0)
        lane = iota((16, 128), 1)
        right = jnp.where(lane == 127, pltpu.roll(to_east, 127, 1), pltpu.roll(own, 127, 1))
        left = jnp.where(lane == 0, pltpu.roll(to_west, 1, 1), pltpu.roll(own, 1, 1))
        u, v, m = own[0:4], own[4:8], own[8:12]
        ur, vr, mr = right[0:4], right[4:8], right[8:12]
        ul, vl, ml = left[0:4], left[4:8], left[8:12]
        ut = jnp.concatenate([to_south[3:4], u, to_north[0:1]], axis=0)
        vt = jnp.concatenate([to_south[7:8], v, to_north[4:5]], axis=0)
        mt = jnp.concatenate([to_south[11:12], m, to_north[8:9]], axis=0)
        fur, ful = 0.5 * (u + ur), 0.5 * (ul + u)
        oxr, oxl = m * mr, ml * m
        fv, oy = 0.5 * (vt[0:5] + vt[1:6]), mt[0:5] * mt[1:6]
        ux, vx = 0.5 * (ur - ul), 0.5 * (vr - vl)
        uy, vy = 0.5 * (ut[2:6] - ut[0:4]), 0.5 * (vt[2:6] - vt[0:4])
        wide = lambda a: jnp.broadcast_to(a, (8, 128))
        for y in range(4):
            for n, a in enumerate((fur, oxr, ful, oxl)):
                face_x[y, n] = wide(a[y : y + 1])
            sea_ref[y] = wide(m[y : y + 1])
        for y in range(5):
            face_y[y, 0] = wide(fv[y : y + 1])
            face_y[y, 1] = wide(oy[y : y + 1])
        for d in range(HALF):
            phi = (d + 1) * 2.0 * math.pi / ND
            fs, fc = math.sin(phi), math.cos(phi)
            turn = TURN_SCALE * ((fs * fc) * (ux - vy) + (fs * fs) * uy - (fc * fc) * vx)
            for y in range(4):
                turn_ref[y, d] = wide(turn[y : y + 1])

    def arrive(c):
        at, width = CHUNKS[c]
        for copy in halo_copies(c):
            copy.wait_recv()
        e_ref[0, at : at + HELD[c], :] = ns_in[c][1].astype(F32)
        e_ref[5, at : at + HELD[c], :] = ns_in[c][0].astype(F32)
        placed = dot(ew_in[c][...].reshape(32, width), place, 0, 0)
        for y in range(4):
            hp_ref[y, at : at + width, :] = placed[:, 128 * y : 128 * (y + 1)]

    lane = iota((8, 128), 1)

    def advance(step, _):
        g, y = step // 4, step % 4
        base = g * GROUP
        cg = table_ref[pl.ds(pl.multiple_of(80 + g * 8, 8), 8), :]
        fur, oxr, ful, oxl = [face_x[y, n] for n in range(4)]
        fvs, oys, fvn, oyn = face_y[y, 0], face_y[y, 1], face_y[y + 1, 0], face_y[y + 1, 1]
        sea = sea_ref[y]

        def flux(speed, here, there, is_open):
            return is_open * (speed * jnp.where(speed > 0.0, here, there))

        moved = []
        for d in range(HALF):
            theta = (d + 0.5) * 2.0 * math.pi / ND
            rows = pl.ds(base + d, 8, stride=HALF)
            here, up, down = e_ref[y + 1, rows, :], e_ref[y + 2, rows, :], e_ref[y, rows, :]
            halo = hp_ref[y, rows, :]
            right = jnp.where(lane == 127, halo, pltpu.roll(here, 127, 1))
            left = jnp.where(lane == 0, halo, pltpu.roll(here, 1, 1))
            sx, sy = cg * math.cos(theta), cg * math.sin(theta)
            div_x = flux(sx + fur, here, right, oxr) - flux(sx + ful, left, here, oxl)
            div_y = flux(sy + fvn, here, up, oyn) - flux(sy + fvs, down, here, oys)
            moved.append(here - div_x - div_y)
        half = iota((8, 128), 0) % 2
        swap = lambda a: jnp.where(half == 0, pltpu.roll(a, 7, 0), pltpu.roll(a, 1, 0))
        first = swap(moved[0])
        bent = []
        for d in range(HALF):
            turn = turn_ref[y, d]
            bent.append(turn * jnp.where(turn > 0.0, moved[d], moved[d + 1] if d + 1 < HALF else first))
        before = swap(bent[-1])
        for d in range(HALF):
            value = (moved[d] - (bent[d] - before)) * sea
            o_ref[pl.ds(g * (4 * GROUP) + d * 4 + y, 8, stride=4 * HALF), :] = value
            before = bent[d]
        return 0

    def finish(g, _):
        rows = pl.ds(pl.multiple_of(g * 4 * GROUP, 16), 4 * GROUP)
        out_ref[rows, :] = o_ref[rows, :].astype(BF16)
        return 0

    def propagate(c):
        first, last = READY_GROUPS[c]
        arrive(c)
        lax.fori_loop(first * 4, last * 4, advance, 0)
        lax.fori_loop(first, last, finish, 0)

    middle(0)
    send1(1)
    drain(cur_all.at[core], c_sem.at[1])
    swap.start()
    middle(2)
    send1(3)
    send_aux()
    middle(1)
    middle(3)
    prepare()
    pick(0)
    pick(1)
    propagate(0)
    pick(2)
    propagate(1)
    pick(3)
    propagate(2)
    propagate(3)

    for c in range(NC):
        drain(x1[c].at[pl.ds(0, SHAPES[FIRST[c]][0] - 1)], p1_send.at[c])
        drain(y2[c].at[pl.ds(0, SHAPES[1 - FIRST[c]][0] - 1)], p2_send.at[c])
        for copy in halo_copies(c):
            copy.wait_send()
    drain(cur_all.at[core, pl.ds(0, NZX - 1)], c_sem.at[0])
    swap.wait_send()
    for copy in aux_copies():
        copy.wait_send()


def tables():
    ratio = 1.1 ** np.arange(NF)
    theta = (np.arange(ND) + 0.5) * 2.0 * np.pi / ND
    table = np.zeros((232, 1))
    table[0:ND, 0] = np.cos(theta)
    table[40 : 40 + ND, 0] = np.sin(theta)
    table[80:152, 0] = np.repeat(0.53 / ratio, 2) * np.tile([1.0, -1.0], NF)
    table[152 : 152 + NF, 0] = ratio / 44.6
    table[192 : 192 + NF, 0] = ratio / ratio[-1]
    return np.repeat(table, 128, axis=1).astype(np.float32)


def body(spec_pts, wind_u, wind_v, ocean_current, block_owner, block_slot, cell_source, land_mask):
    hbm = pl.BlockSpec(memory_space=pltpu.HBM)
    per_chunk = lambda shape: [pltpu.VMEM(shape(i, w), BF16) for i, w in enumerate(WIDTHS)]
    dma = pltpu.SemaphoreType.DMA
    out = pl.pallas_call(
        kernel,
        out_shape=jax.ShapeDtypeStruct((SPEC * 4, 128), BF16),
        in_specs=[hbm] * 9,
        out_specs=pl.BlockSpec(memory_space=pltpu.VMEM),
        scratch_shapes=[
            pltpu.VMEM((NF, ND, CELLS), BF16),
            pltpu.VMEM((1, CELLS), F32),
            pltpu.VMEM((1, CELLS), F32),
            pltpu.VMEM((232, 128), F32),
            pltpu.VMEM((1, 4), jnp.int32),
            pltpu.VMEM((1, 4), jnp.int32),
            pltpu.VMEM((4, 128), jnp.int32),
            pltpu.VMEM((4, 128), jnp.int32),
            pltpu.VMEM((PAD, CELLS), F32),
            pltpu.VMEM((6, PAD, 128), F32),
            pltpu.VMEM((4, PAD, 128), F32),
            pltpu.VMEM((SPEC * 4, 128), F32),
            per_chunk(lambda i, w: (*SHAPES[FIRST[i]], w)),
            per_chunk(lambda i, w: (*SHAPES[FIRST[i]], w)),
            per_chunk(lambda i, w: (*SHAPES[1 - FIRST[i]], w)),
            per_chunk(lambda i, w: (*SHAPES[1 - FIRST[i]], w)),
            per_chunk(lambda i, w: (2, HELD[i], 128)),
            per_chunk(lambda i, w: (2, HELD[i], 128)),
            per_chunk(lambda i, w: (16, w)),
            per_chunk(lambda i, w: (2, 16, w)),
            pltpu.VMEM((2, NZX, 16, 128), BF16),
            pltpu.VMEM((16, 128), BF16),
            pltpu.VMEM((4, 16, 128), BF16),
            pltpu.VMEM((4, 4, 8, 128), F32),
            pltpu.VMEM((5, 2, 8, 128), F32),
            pltpu.VMEM((4, HALF, 8, 128), F32),
            pltpu.VMEM((4, 8, 128), F32),
            pltpu.VMEM((2, CELLS, CELLS), BF16),
            dma((NC,)), dma((NC,)), dma((NC,)), dma((NC,)), dma((NC, 4)), dma((NC, 4)), dma((4,)), dma((4,)), dma((4,)),
            dma((LOADS + 7,)),
        ],
        compiler_params=pltpu.CompilerParams(
            collective_id=0, has_side_effects=True, vmem_limit_bytes=50 * 2**20
        ),
    )(*[
        pltpu.with_memory_space_constraint(a, pltpu.HBM)
        for a in (
            spec_pts, wind_u.reshape(1, CELLS), wind_v.reshape(1, CELLS), jnp.asarray(tables()),
            ocean_current.reshape(16, 128), block_owner.T, block_slot.T, cell_source, land_mask,
        )
    ])
    return out.reshape(NF, ND, 4, 128)


def solution(mesh):
    return jax.shard_map(
        body,
        mesh=mesh,
        in_specs=(
            P(None, None, ("lon", "lat")),
            P(("lon", "lat")),
            P(("lon", "lat")),
            P(None, "lat", "lon", None),
            P("lat", "lon"),
            P("lat", "lon"),
            P("lat", "lon"),
            P("lat", "lon"),
        ),
        out_specs=P(None, None, "lat", "lon"),
        check_vma=False,
    )
```

```python
import functools
import math

import jax
import jax.numpy as jnp
import numpy as np
from jax import lax
from jax.experimental import pallas as pl
from jax.experimental.pallas import tpu as pltpu
from jax.sharding import PartitionSpec as P

NF, ND = 36, 36
SPEC = NF * ND
PAD = 1408
CELLS = 512
NK, NZX = 16, 32
WIDTHS = (384, 384, 512, 128)
FIRST = (1, 1, 0, 0)
CHUNKS = tuple((sum(WIDTHS[:i]), w) for i, w in enumerate(WIDTHS))
SHAPES = ((NK, NZX), (NZX, NK))
HELD = tuple(min(w, SPEC - at) for at, w in CHUNKS)
NC = len(CHUNKS)
LOADS = 4
GROUP = 4 * ND


def spans(counts):
    return tuple(zip((0,) + counts[:-1], counts))


READY_GROUPS = spans(tuple(min((at + w) // GROUP, SPEC // GROUP) for at, w in CHUNKS))
HALF = ND // 2
MESH = pl.DeviceIdType.MESH
TURN_SCALE = 2.5
F32, BF16 = jnp.float32, jnp.bfloat16


def iota(shape, axis):
    return lax.broadcasted_iota(jnp.int32, shape, axis)


def onehot(cond):
    return jnp.where(cond, 1.0, 0.0).astype(BF16)


def dot(a, b, ca, cb):
    return lax.dot_general(a, b, (((ca,), (cb,)), ((), ())), preferred_element_type=F32)


def drain(ref, sem):
    pltpu.make_async_copy(ref, ref, sem).wait()


def kernel(
    spec_hbm, wu_hbm, wv_hbm, table_hbm, cur_ref, owner_hbm, slot_hbm, source_hbm, mask_hbm,
    out_ref,
    spec_ref, wu_ref, wv_ref, table_ref, owner_ref, slot_ref, source_ref, mask_ref,
    s_ref, e_ref, hp_ref, o_ref, x1, y1, y2, z, ns_out, ns_in, ew_out, ew_in, cur_all, aux_out, aux_in,
    face_x, face_y, turn_ref, sea_ref, pick_ref,
    p1_send, p1_recv, p2_send, p2_recv, h_send, h_recv, c_sem, a_send, a_recv, in_sem,
):
    lon, lat = lax.axis_index("lon"), lax.axis_index("lat")
    n_lon, n_lat = NZX * 2, NK // 2
    zx, core = lon // 2, lon % 2
    me = lat * 2 + core
    north, south = (lat + 1) % n_lat, (lat + n_lat - 1) % n_lat
    east, west = (lon + 1) % n_lon, (lon + n_lon - 1) % n_lon
    sides = ((lon, north), (lon, south), (east, lat), (west, lat))

    def dev(lo, la):
        return {"lon": lo, "lat": la}

    small = (
        (wu_hbm, wu_ref), (wv_hbm, wv_ref), (table_hbm, table_ref), (owner_hbm, owner_ref), (slot_hbm, slot_ref),
        (source_hbm, source_ref), (mask_hbm, mask_ref),
    )
    parts = [pl.ds(i * (NF // LOADS), NF // LOADS) for i in range(LOADS)]
    loads = [pltpu.make_async_copy(spec_hbm.at[p], spec_ref.at[p], in_sem.at[i]) for i, p in enumerate(parts)]
    loads += [pltpu.make_async_copy(a, b, in_sem.at[LOADS + i]) for i, (a, b) in enumerate(small)]
    for load in loads:
        load.start()
    barrier = pltpu.get_barrier_semaphore()

    def greet1(i, _):
        k = (me + i) % NK
        pl.semaphore_signal(barrier, inc=1, device_id=dev(zx * 2 + k % 2, k // 2), device_id_type=MESH)
        return 0

    def greet2(i, _):
        t = (zx + i) % NZX
        pl.semaphore_signal(barrier, inc=1, device_id=dev(t * 2 + core, lat), device_id_type=MESH)
        return 0

    lax.fori_loop(1, NK, greet1, 0)
    lax.fori_loop(1, NZX, greet2, 0)
    for lo, la in ((east, lat), (west, lat)):
        pl.semaphore_signal(barrier, inc=1, device_id=dev(lo, la), device_id_type=MESH)

    def add(f, acc):
        return acc + spec_ref[f].astype(F32)

    total = jnp.zeros((ND, CELLS), F32)
    for i in range(LOADS):
        loads[i].wait()
        total = lax.fori_loop(i * (NF // LOADS), (i + 1) * (NF // LOADS), add, total)
    for load in loads[LOADS:]:
        load.wait()
    m0 = jnp.sum(total, axis=0, keepdims=True) / SPEC
    loss0 = 0.3 * (m0 / 0.5) ** 2
    across = lambda a: jnp.concatenate([a] * 4, axis=1)
    proj = wu_ref[...] * across(table_ref[0:ND, :]) + wv_ref[...] * across(table_ref[40 : 40 + ND, :])
    s_ref[SPEC:PAD, :] = jnp.zeros((PAD - SPEC, CELLS), F32)

    row, col = iota((CELLS, CELLS), 0), iota((CELLS, CELLS), 1)
    by_dest, regroup = [], []
    for rows_of, columns_of in (SHAPES, SHAPES[::-1]):
        minor, other = rows_of[1], columns_of[1]
        major, rest = row // minor, row % minor
        k, t = (major, rest) if minor == NZX else (rest, major)
        by_dest.append(onehot(col == (k // 2) * n_lon + t * 2 + k % 2))
        regroup.append(onehot((row // other == col % minor) & (row % other == col // minor)))

    def source(g, _):
        rows = s_ref.at[pl.ds(pl.multiple_of(g * GROUP, 16), GROUP), :]
        for i in range(4):
            f = g * 4 + i
            per_speed = across(table_ref[pl.ds(152 + f, 1), :])
            rel = across(table_ref[pl.ds(192 + f, 1), :])
            drive = jnp.maximum(proj * per_speed - 1.0, 0.0)
            gain = 0.5 * jnp.tanh(0.2 * drive)
            rows[ND * i : ND * (i + 1), :] = spec_ref[f].astype(F32) * jnp.exp(gain - rel * loss0)
        return 0

    def exchange(axis, src, dst, send, recv):
        n, mine = ((NK, me), (NZX, zx))[axis]

        def one(i, _):
            to = (mine + i) % n
            pltpu.make_async_remote_copy(
                src_ref=src.at[to], dst_ref=dst.at[mine], send_sem=send, recv_sem=recv,
                device_id=(dev(zx * 2 + to % 2, to // 2), dev(to * 2 + core, lat))[axis], device_id_type=MESH,
            ).start()
            return 0

        lax.fori_loop(1, n, one, 0)
        pltpu.make_async_copy(src.at[mine], dst.at[mine], recv).start()

    def send1(c):
        exchange(FIRST[c], x1[c], y1[c], p1_send.at[c], p1_recv.at[c])

    def send2(c):
        exchange(1 - FIRST[c], y2[c], z[c], p2_send.at[c], p2_recv.at[c])

    def dispatch(c):
        at, width = CHUNKS[c]
        values = s_ref[at : at + width, :].astype(BF16)
        x1[c][...] = dot(by_dest[FIRST[c]], values, 1, 1).astype(BF16).reshape(*SHAPES[FIRST[c]], width)

    def middle(c):
        width = CHUNKS[c][1]
        drain(y1[c], p1_recv.at[c])
        values = dot(regroup[FIRST[c]], y1[c][...].reshape(CELLS, width), 1, 0)
        y2[c][...] = values.astype(BF16).reshape(*SHAPES[1 - FIRST[c]], width)
        send2(c)

    def share(i, _):
        t = (zx + i) % NZX
        pltpu.make_async_remote_copy(
            src_ref=cur_ref, dst_ref=cur_all.at[core, zx], send_sem=c_sem.at[0], recv_sem=c_sem.at[1],
            device_id=dev(t * 2 + core, lat), device_id_type=MESH,
        ).start()
        return 0

    swap = pltpu.make_async_remote_copy(
        src_ref=cur_all.at[core], dst_ref=cur_all.at[core], send_sem=c_sem.at[2], recv_sem=c_sem.at[3],
        device_id=dev(zx * 2 + 1 - core, lat), device_id_type=MESH,
    )

    first_groups = -(-WIDTHS[0] // GROUP)
    lax.fori_loop(0, first_groups, source, 0)
    dispatch(0)
    pl.semaphore_wait(barrier, NK - 1 + NZX - 1 + 2)
    send1(0)
    lax.fori_loop(first_groups, SPEC // GROUP, source, 0)
    dispatch(2)
    send1(2)
    lax.fori_loop(1, NZX, share, 0)
    pltpu.make_async_copy(cur_ref, cur_all.at[core, zx], c_sem.at[1]).start()
    dispatch(1)
    dispatch(3)

    q = source_ref[...]
    from_k, from_t = (q // n_lon) * 2 + q % 2, (q % n_lon) // 2
    slots = iota((CELLS, 128), 0)
    edge_row = iota((16, 1), 0)
    edge_pick = []
    for kind, where in enumerate((from_t * NK + from_k, from_k * NZX + from_t)):
        where = jnp.where(mask_ref[...] > 0, where, -1)
        for y in range(4):
            pick_ref[kind, :, 128 * y : 128 * (y + 1)] = onehot(slots == where[y : y + 1, :])
        both = jnp.concatenate([where, where, jnp.full((8, 128), -1, jnp.int32)], axis=0)
        edge = jnp.where(edge_row < 4, both[:, 127:128], both[:, 0:1])
        edge_pick.append(onehot(iota((16, CELLS), 1) == edge))
    pr, pc = iota((32, CELLS), 0), iota((32, CELLS), 1)
    place = onehot(((pr < 4) & (pc == pr * 128)) | ((pr >= 20) & (pr < 24) & (pc == (pr - 20) * 128 + 127)))

    def halo_copies(c):
        ew = (ew_out[c], ew_in[c])
        ns = (ns_out[c], ns_in[c])
        parts = (
            (ns[0].at[1], ns[1].at[1]),
            (ns[0].at[0], ns[1].at[0]),
            (ew[0], ew[1].at[0]),
            (ew[0], ew[1].at[1]),
        )
        return [
            pltpu.make_async_remote_copy(
                src_ref=src, dst_ref=dst, send_sem=h_send.at[c, d], recv_sem=h_recv.at[c, d],
                device_id=dev(*sides[d]), device_id_type=MESH,
            )
            for d, (src, dst) in enumerate(parts)
        ]

    def aux_copies():
        return [
            pltpu.make_async_remote_copy(
                src_ref=aux_out, dst_ref=aux_in.at[d], send_sem=a_send.at[d], recv_sem=a_recv.at[d],
                device_id=dev(*sides[d]), device_id_type=MESH,
            )
            for d in range(4)
        ]

    def pick(c):
        at, width = CHUNKS[c]
        drain(z[c], p2_recv.at[c])
        got = z[c][...].reshape(CELLS, width)
        ew_out[c][...] = dot(edge_pick[FIRST[c]], got, 1, 0).astype(BF16)
        energy = dot(got, pick_ref[FIRST[c]], 0, 0)
        for y in range(4):
            e_ref[1 + y, at : at + width, :] = energy[:, 128 * y : 128 * (y + 1)]
        ns_out[c][0] = energy[: HELD[c], :128].astype(BF16)
        ns_out[c][1] = energy[: HELD[c], 384:].astype(BF16)
        for copy in halo_copies(c):
            copy.start()

    def send_aux():
        swap.wait_recv()
        owner = owner_ref[...]
        wanted = ((owner % 2) * NZX + owner // 2) * 16 + slot_ref[...]
        r, n = iota((16, 4), 0), iota((16, 4), 1)
        wanted = jnp.where(r % 4 == n, wanted + 8 * (r // 4), 0).astype(F32)
        wanted = jnp.sum(wanted, axis=1, keepdims=True).astype(jnp.int32)
        wanted = jnp.where(iota((16, 1), 0) < 8, wanted, -1)
        blocks = onehot(iota((16, NZX * 32), 1) == wanted)
        found = dot(blocks, cur_all[...].reshape(NZX * 32, 128), 1, 0)
        sea = jnp.concatenate([jnp.zeros((8, 128), F32), mask_ref[...].astype(F32), jnp.zeros((4, 128), F32)], axis=0)
        aux_out[...] = (found + sea).astype(BF16)
        for copy in aux_copies():
            copy.start()

    def prepare():
        for copy in aux_copies():
            copy.wait_recv()
        own = aux_out[...].astype(F32)
        to_south, to_north, to_west, to_east = [aux_in[d].astype(F32) for d in range(4)]
        to_north = to_north * jnp.where(lat < n_lat - 1, 1.0, 0.0)
        to_south = to_south * jnp.where(lat > 0, 1.0, 0.0)
        lane = iota((16, 128), 1)
        right = jnp.where(lane == 127, pltpu.roll(to_east, 127, 1), pltpu.roll(own, 127, 1))
        left = jnp.where(lane == 0, pltpu.roll(to_west, 1, 1), pltpu.roll(own, 1, 1))
        u, v, m = own[0:4], own[4:8], own[8:12]
        ur, vr, mr = right[0:4], right[4:8], right[8:12]
        ul, vl, ml = left[0:4], left[4:8], left[8:12]
        ut = jnp.concatenate([to_south[3:4], u, to_north[0:1]], axis=0)
        vt = jnp.concatenate([to_south[7:8], v, to_north[4:5]], axis=0)
        mt = jnp.concatenate([to_south[11:12], m, to_north[8:9]], axis=0)
        fur, ful = 0.5 * (u + ur), 0.5 * (ul + u)
        oxr, oxl = m * mr, ml * m
        fv, oy = 0.5 * (vt[0:5] + vt[1:6]), mt[0:5] * mt[1:6]
        ux, vx = 0.5 * (ur - ul), 0.5 * (vr - vl)
        uy, vy = 0.5 * (ut[2:6] - ut[0:4]), 0.5 * (vt[2:6] - vt[0:4])
        wide = lambda a: jnp.broadcast_to(a, (8, 128))
        for y in range(4):
            for n, a in enumerate((fur, oxr, ful, oxl)):
                face_x[y, n] = wide(a[y : y + 1])
            sea_ref[y] = wide(m[y : y + 1])
        for y in range(5):
            face_y[y, 0] = wide(fv[y : y + 1])
            face_y[y, 1] = wide(oy[y : y + 1])
        for d in range(HALF):
            phi = (d + 1) * 2.0 * math.pi / ND
            fs, fc = math.sin(phi), math.cos(phi)
            turn = TURN_SCALE * ((fs * fc) * (ux - vy) + (fs * fs) * uy - (fc * fc) * vx)
            for y in range(4):
                turn_ref[y, d] = wide(turn[y : y + 1])

    def arrive(c):
        at, width = CHUNKS[c]
        for copy in halo_copies(c):
            copy.wait_recv()
        e_ref[0, at : at + HELD[c], :] = ns_in[c][1].astype(F32)
        e_ref[5, at : at + HELD[c], :] = ns_in[c][0].astype(F32)
        placed = dot(ew_in[c][...].reshape(32, width), place, 0, 0)
        for y in range(4):
            hp_ref[y, at : at + width, :] = placed[:, 128 * y : 128 * (y + 1)]

    lane = iota((8, 128), 1)

    def advance(step, _):
        g, y = step // 4, step % 4
        base = g * GROUP
        cg = table_ref[pl.ds(pl.multiple_of(80 + g * 8, 8), 8), :]
        fur, oxr, ful, oxl = [face_x[y, n] for n in range(4)]
        fvs, oys, fvn, oyn = face_y[y, 0], face_y[y, 1], face_y[y + 1, 0], face_y[y + 1, 1]
        sea = sea_ref[y]

        def flux(speed, here, there, is_open):
            return is_open * (speed * jnp.where(speed > 0.0, here, there))

        moved = []
        for d in range(HALF):
            theta = (d + 0.5) * 2.0 * math.pi / ND
            rows = pl.ds(base + d, 8, stride=HALF)
            here, up, down = e_ref[y + 1, rows, :], e_ref[y + 2, rows, :], e_ref[y, rows, :]
            halo = hp_ref[y, rows, :]
            right = jnp.where(lane == 127, halo, pltpu.roll(here, 127, 1))
            left = jnp.where(lane == 0, halo, pltpu.roll(here, 1, 1))
            sx, sy = cg * math.cos(theta), cg * math.sin(theta)
            div_x = flux(sx + fur, here, right, oxr) - flux(sx + ful, left, here, oxl)
            div_y = flux(sy + fvn, here, up, oyn) - flux(sy + fvs, down, here, oys)
            moved.append(here - div_x - div_y)
        half = iota((8, 128), 0) % 2
        swap = lambda a: jnp.where(half == 0, pltpu.roll(a, 7, 0), pltpu.roll(a, 1, 0))
        first = swap(moved[0])
        bent = []
        for d in range(HALF):
            turn = turn_ref[y, d]
            bent.append(turn * jnp.where(turn > 0.0, moved[d], moved[d + 1] if d + 1 < HALF else first))
        before = swap(bent[-1])
        for d in range(HALF):
            value = (moved[d] - (bent[d] - before)) * sea
            o_ref[pl.ds(g * (4 * GROUP) + d * 4 + y, 8, stride=4 * HALF), :] = value
            before = bent[d]
        return 0

    def finish(g, _):
        rows = pl.ds(pl.multiple_of(g * 4 * GROUP, 16), 4 * GROUP)
        out_ref[rows, :] = o_ref[rows, :].astype(BF16)
        return 0

    def propagate(c):
        first, last = READY_GROUPS[c]
        arrive(c)
        lax.fori_loop(first * 4, last * 4, advance, 0)
        lax.fori_loop(first, last, finish, 0)

    middle(0)
    send1(1)
    drain(cur_all.at[core], c_sem.at[1])
    swap.start()
    middle(2)
    send1(3)
    send_aux()
    middle(1)
    middle(3)
    prepare()
    pick(0)
    pick(1)
    propagate(0)
    pick(2)
    propagate(1)
    pick(3)
    propagate(2)
    propagate(3)

    for c in range(NC):
        drain(x1[c].at[pl.ds(0, SHAPES[FIRST[c]][0] - 1)], p1_send.at[c])
        drain(y2[c].at[pl.ds(0, SHAPES[1 - FIRST[c]][0] - 1)], p2_send.at[c])
        for copy in halo_copies(c):
            copy.wait_send()
    drain(cur_all.at[core, pl.ds(0, NZX - 1)], c_sem.at[0])
    swap.wait_send()
    for copy in aux_copies():
        copy.wait_send()


def tables():
    ratio = 1.1 ** np.arange(NF)
    theta = (np.arange(ND) + 0.5) * 2.0 * np.pi / ND
    table = np.zeros((232, 1))
    table[0:ND, 0] = np.cos(theta)
    table[40 : 40 + ND, 0] = np.sin(theta)
    table[80:152, 0] = np.repeat(0.53 / ratio, 2) * np.tile([1.0, -1.0], NF)
    table[152 : 152 + NF, 0] = ratio / 44.6
    table[192 : 192 + NF, 0] = ratio / ratio[-1]
    return np.repeat(table, 128, axis=1).astype(np.float32)


def body(spec_pts, wind_u, wind_v, ocean_current, block_owner, block_slot, cell_source, land_mask):
    hbm = pl.BlockSpec(memory_space=pltpu.HBM)
    per_chunk = lambda shape: [pltpu.VMEM(shape(i, w), BF16) for i, w in enumerate(WIDTHS)]
    dma = pltpu.SemaphoreType.DMA
    out = pl.pallas_call(
        kernel,
        out_shape=jax.ShapeDtypeStruct((SPEC * 4, 128), BF16),
        in_specs=[hbm] * 9,
        out_specs=pl.BlockSpec(memory_space=pltpu.VMEM),
        scratch_shapes=[
            pltpu.VMEM((NF, ND, CELLS), BF16),
            pltpu.VMEM((1, CELLS), F32),
            pltpu.VMEM((1, CELLS), F32),
            pltpu.VMEM((232, 128), F32),
            pltpu.VMEM((1, 4), jnp.int32),
            pltpu.VMEM((1, 4), jnp.int32),
            pltpu.VMEM((4, 128), jnp.int32),
            pltpu.VMEM((4, 128), jnp.int32),
            pltpu.VMEM((PAD, CELLS), F32),
            pltpu.VMEM((6, PAD, 128), F32),
            pltpu.VMEM((4, PAD, 128), F32),
            pltpu.VMEM((SPEC * 4, 128), F32),
            per_chunk(lambda i, w: (*SHAPES[FIRST[i]], w)),
            per_chunk(lambda i, w: (*SHAPES[FIRST[i]], w)),
            per_chunk(lambda i, w: (*SHAPES[1 - FIRST[i]], w)),
            per_chunk(lambda i, w: (*SHAPES[1 - FIRST[i]], w)),
            per_chunk(lambda i, w: (2, HELD[i], 128)),
            per_chunk(lambda i, w: (2, HELD[i], 128)),
            per_chunk(lambda i, w: (16, w)),
            per_chunk(lambda i, w: (2, 16, w)),
            pltpu.VMEM((2, NZX, 16, 128), BF16),
            pltpu.VMEM((16, 128), BF16),
            pltpu.VMEM((4, 16, 128), BF16),
            pltpu.VMEM((4, 4, 8, 128), F32),
            pltpu.VMEM((5, 2, 8, 128), F32),
            pltpu.VMEM((4, HALF, 8, 128), F32),
            pltpu.VMEM((4, 8, 128), F32),
            pltpu.VMEM((2, CELLS, CELLS), BF16),
            dma((NC,)), dma((NC,)), dma((NC,)), dma((NC,)), dma((NC, 4)), dma((NC, 4)), dma((4,)), dma((4,)), dma((4,)),
            dma((LOADS + 7,)),
        ],
        compiler_params=pltpu.CompilerParams(
            collective_id=0, has_side_effects=True, vmem_limit_bytes=50 * 2**20
        ),
    )(*[
        pltpu.with_memory_space_constraint(a, pltpu.HBM)
        for a in (
            spec_pts, wind_u.reshape(1, CELLS), wind_v.reshape(1, CELLS), jnp.asarray(tables()),
            ocean_current.reshape(16, 128), block_owner.T, block_slot.T, cell_source, land_mask,
        )
    ])
    return out.reshape(NF, ND, 4, 128)


def solution(mesh):
    return jax.shard_map(
        body,
        mesh=mesh,
        in_specs=(
            P(None, None, ("lon", "lat")),
            P(("lon", "lat")),
            P(("lon", "lat")),
            P(None, "lat", "lon", None),
            P("lat", "lon"),
            P("lat", "lon"),
            P("lat", "lon"),
            P("lat", "lon"),
        ),
        out_specs=P(None, None, "lat", "lon"),
        check_vma=False,
    )
```

```python
import functools
import math

import jax
import jax.numpy as jnp
import numpy as np
from jax import lax
from jax.experimental import pallas as pl
from jax.experimental.pallas import tpu as pltpu
from jax.sharding import PartitionSpec as P

NF, ND = 36, 36
SPEC = NF * ND
PAD = 1408
CELLS = 512
NK, NZX = 16, 32
WIDTHS = (384, 384, 512, 128)
FIRST = (1, 1, 0, 0)
CHUNKS = tuple((sum(WIDTHS[:i]), w) for i, w in enumerate(WIDTHS))
SHAPES = ((NK, NZX), (NZX, NK))
HELD = tuple(min(w, SPEC - at) for at, w in CHUNKS)
NC = len(CHUNKS)
LOADS = 4
GROUP = 4 * ND


def spans(counts):
    return tuple(zip((0,) + counts[:-1], counts))


READY_GROUPS = spans(tuple(min((at + w) // GROUP, SPEC // GROUP) for at, w in CHUNKS))
HALF = ND // 2
MESH = pl.DeviceIdType.MESH
TURN_SCALE = 2.5
F32, BF16 = jnp.float32, jnp.bfloat16


def iota(shape, axis):
    return lax.broadcasted_iota(jnp.int32, shape, axis)


def onehot(cond):
    return jnp.where(cond, 1.0, 0.0).astype(BF16)


def dot(a, b, ca, cb):
    return lax.dot_general(a, b, (((ca,), (cb,)), ((), ())), preferred_element_type=F32)


def drain(ref, sem):
    pltpu.make_async_copy(ref, ref, sem).wait()


def kernel(
    spec_hbm, wu_hbm, wv_hbm, table_hbm, cur_ref, owner_hbm, slot_hbm, source_hbm, mask_hbm,
    out_ref,
    spec_ref, wu_ref, wv_ref, table_ref, owner_ref, slot_ref, source_ref, mask_ref,
    s_ref, e_ref, hp_ref, o_ref, x1, y1, y2, z, ns_out, ns_in, ew_out, ew_in, cur_all, aux_out, aux_in,
    face_x, face_y, turn_ref, sea_ref, pick_ref,
    p1_send, p1_recv, p2_send, p2_recv, h_send, h_recv, c_sem, a_send, a_recv, in_sem,
):
    lon, lat = lax.axis_index("lon"), lax.axis_index("lat")
    n_lon, n_lat = NZX * 2, NK // 2
    zx, core = lon // 2, lon % 2
    me = lat * 2 + core
    north, south = (lat + 1) % n_lat, (lat + n_lat - 1) % n_lat
    east, west = (lon + 1) % n_lon, (lon + n_lon - 1) % n_lon
    sides = ((lon, north), (lon, south), (east, lat), (west, lat))

    def dev(lo, la):
        return {"lon": lo, "lat": la}

    small = (
        (wu_hbm, wu_ref), (wv_hbm, wv_ref), (table_hbm, table_ref), (owner_hbm, owner_ref), (slot_hbm, slot_ref),
        (source_hbm, source_ref), (mask_hbm, mask_ref),
    )
    parts = [pl.ds(i * (NF // LOADS), NF // LOADS) for i in range(LOADS)]
    loads = [pltpu.make_async_copy(spec_hbm.at[p], spec_ref.at[p], in_sem.at[i]) for i, p in enumerate(parts)]
    loads += [pltpu.make_async_copy(a, b, in_sem.at[LOADS + i]) for i, (a, b) in enumerate(small)]
    for load in loads:
        load.start()
    barrier = pltpu.get_barrier_semaphore()

    def greet1(i, _):
        k = (me + i) % NK
        pl.semaphore_signal(barrier, inc=1, device_id=dev(zx * 2 + k % 2, k // 2), device_id_type=MESH)
        return 0

    def greet2(i, _):
        t = (zx + i) % NZX
        pl.semaphore_signal(barrier, inc=1, device_id=dev(t * 2 + core, lat), device_id_type=MESH)
        return 0

    lax.fori_loop(1, NK, greet1, 0)
    lax.fori_loop(1, NZX, greet2, 0)
    for lo, la in ((east, lat), (west, lat)):
        pl.semaphore_signal(barrier, inc=1, device_id=dev(lo, la), device_id_type=MESH)

    def add(f, acc):
        return acc + spec_ref[f].astype(F32)

    total = jnp.zeros((ND, CELLS), F32)
    for i in range(LOADS):
        loads[i].wait()
        total = lax.fori_loop(i * (NF // LOADS), (i + 1) * (NF // LOADS), add, total)
    for load in loads[LOADS:]:
        load.wait()
    m0 = jnp.sum(total, axis=0, keepdims=True) / SPEC
    loss0 = 0.3 * (m0 / 0.5) ** 2
    across = lambda a: jnp.concatenate([a] * 4, axis=1)
    proj = wu_ref[...] * across(table_ref[0:ND, :]) + wv_ref[...] * across(table_ref[40 : 40 + ND, :])
    s_ref[SPEC:PAD, :] = jnp.zeros((PAD - SPEC, CELLS), F32)

    row, col = iota((CELLS, CELLS), 0), iota((CELLS, CELLS), 1)
    by_dest, regroup = [], []
    for rows_of, columns_of in (SHAPES, SHAPES[::-1]):
        minor, other = rows_of[1], columns_of[1]
        major, rest = row // minor, row % minor
        k, t = (major, rest) if minor == NZX else (rest, major)
        by_dest.append(onehot(col == (k // 2) * n_lon + t * 2 + k % 2))
        regroup.append(onehot((row // other == col % minor) & (row % other == col // minor)))

    def source(g, _):
        rows = s_ref.at[pl.ds(pl.multiple_of(g * GROUP, 16), GROUP), :]
        for i in range(4):
            f = g * 4 + i
            per_speed = across(table_ref[pl.ds(152 + f, 1), :])
            rel = across(table_ref[pl.ds(192 + f, 1), :])
            drive = jnp.maximum(proj * per_speed - 1.0, 0.0)
            gain = 0.5 * jnp.tanh(0.2 * drive)
            rows[ND * i : ND * (i + 1), :] = spec_ref[f].astype(F32) * jnp.exp(gain - rel * loss0)
        return 0

    def exchange(axis, src, dst, send, recv):
        n, mine = ((NK, me), (NZX, zx))[axis]

        def one(i, _):
            to = (mine + i) % n
            pltpu.make_async_remote_copy(
                src_ref=src.at[to], dst_ref=dst.at[mine], send_sem=send, recv_sem=recv,
                device_id=(dev(zx * 2 + to % 2, to // 2), dev(to * 2 + core, lat))[axis], device_id_type=MESH,
            ).start()
            return 0

        lax.fori_loop(1, n, one, 0)
        pltpu.make_async_copy(src.at[mine], dst.at[mine], recv).start()

    def send1(c):
        exchange(FIRST[c], x1[c], y1[c], p1_send.at[c], p1_recv.at[c])

    def send2(c):
        exchange(1 - FIRST[c], y2[c], z[c], p2_send.at[c], p2_recv.at[c])

    def dispatch(c):
        at, width = CHUNKS[c]
        values = s_ref[at : at + width, :].astype(BF16)
        x1[c][...] = dot(by_dest[FIRST[c]], values, 1, 1).astype(BF16).reshape(*SHAPES[FIRST[c]], width)

    def middle(c):
        width = CHUNKS[c][1]
        drain(y1[c], p1_recv.at[c])
        values = dot(regroup[FIRST[c]], y1[c][...].reshape(CELLS, width), 1, 0)
        y2[c][...] = values.astype(BF16).reshape(*SHAPES[1 - FIRST[c]], width)
        send2(c)

    def share(i, _):
        t = (zx + i) % NZX
        pltpu.make_async_remote_copy(
            src_ref=cur_ref, dst_ref=cur_all.at[core, zx], send_sem=c_sem.at[0], recv_sem=c_sem.at[1],
            device_id=dev(t * 2 + core, lat), device_id_type=MESH,
        ).start()
        return 0

    swap = pltpu.make_async_remote_copy(
        src_ref=cur_all.at[core], dst_ref=cur_all.at[core], send_sem=c_sem.at[2], recv_sem=c_sem.at[3],
        device_id=dev(zx * 2 + 1 - core, lat), device_id_type=MESH,
    )

    first_groups = -(-WIDTHS[0] // GROUP)
    lax.fori_loop(0, first_groups, source, 0)
    dispatch(0)
    pl.semaphore_wait(barrier, NK - 1 + NZX - 1 + 2)
    send1(0)
    lax.fori_loop(first_groups, SPEC // GROUP, source, 0)
    dispatch(2)
    send1(2)
    lax.fori_loop(1, NZX, share, 0)
    pltpu.make_async_copy(cur_ref, cur_all.at[core, zx], c_sem.at[1]).start()
    dispatch(1)
    dispatch(3)

    q = source_ref[...]
    from_k, from_t = (q // n_lon) * 2 + q % 2, (q % n_lon) // 2
    slots = iota((CELLS, 128), 0)
    edge_row = iota((16, 1), 0)
    edge_pick = []
    for kind, where in enumerate((from_t * NK + from_k, from_k * NZX + from_t)):
        where = jnp.where(mask_ref[...] > 0, where, -1)
        for y in range(4):
            pick_ref[kind, :, 128 * y : 128 * (y + 1)] = onehot(slots == where[y : y + 1, :])
        both = jnp.concatenate([where, where, jnp.full((8, 128), -1, jnp.int32)], axis=0)
        edge = jnp.where(edge_row < 4, both[:, 127:128], both[:, 0:1])
        edge_pick.append(onehot(iota((16, CELLS), 1) == edge))
    pr, pc = iota((32, CELLS), 0), iota((32, CELLS), 1)
    place = onehot(((pr < 4) & (pc == pr * 128)) | ((pr >= 20) & (pr < 24) & (pc == (pr - 20) * 128 + 127)))

    def halo_copies(c):
        ew = (ew_out[c], ew_in[c])
        ns = (ns_out[c], ns_in[c])
        parts = (
            (ns[0].at[1], ns[1].at[1]),
            (ns[0].at[0], ns[1].at[0]),
            (ew[0], ew[1].at[0]),
            (ew[0], ew[1].at[1]),
        )
        return [
            pltpu.make_async_remote_copy(
                src_ref=src, dst_ref=dst, send_sem=h_send.at[c, d], recv_sem=h_recv.at[c, d],
                device_id=dev(*sides[d]), device_id_type=MESH,
            )
            for d, (src, dst) in enumerate(parts)
        ]

    def aux_copies():
        return [
            pltpu.make_async_remote_copy(
                src_ref=aux_out, dst_ref=aux_in.at[d], send_sem=a_send.at[d], recv_sem=a_recv.at[d],
                device_id=dev(*sides[d]), device_id_type=MESH,
            )
            for d in range(4)
        ]

    def pick(c):
        at, width = CHUNKS[c]
        drain(z[c], p2_recv.at[c])
        got = z[c][...].reshape(CELLS, width)
        ew_out[c][...] = dot(edge_pick[FIRST[c]], got, 1, 0).astype(BF16)
        energy = dot(got, pick_ref[FIRST[c]], 0, 0)
        for y in range(4):
            e_ref[1 + y, at : at + width, :] = energy[:, 128 * y : 128 * (y + 1)]
        ns_out[c][0] = energy[: HELD[c], :128].astype(BF16)
        ns_out[c][1] = energy[: HELD[c], 384:].astype(BF16)
        for copy in halo_copies(c):
            copy.start()

    def send_aux():
        swap.wait_recv()
        owner = owner_ref[...]
        wanted = ((owner % 2) * NZX + owner // 2) * 16 + slot_ref[...]
        r, n = iota((16, 4), 0), iota((16, 4), 1)
        wanted = jnp.where(r % 4 == n, wanted + 8 * (r // 4), 0).astype(F32)
        wanted = jnp.sum(wanted, axis=1, keepdims=True).astype(jnp.int32)
        wanted = jnp.where(iota((16, 1), 0) < 8, wanted, -1)
        blocks = onehot(iota((16, NZX * 32), 1) == wanted)
        found = dot(blocks, cur_all[...].reshape(NZX * 32, 128), 1, 0)
        sea = jnp.concatenate([jnp.zeros((8, 128), F32), mask_ref[...].astype(F32), jnp.zeros((4, 128), F32)], axis=0)
        aux_out[...] = (found + sea).astype(BF16)
        for copy in aux_copies():
            copy.start()

    def prepare():
        for copy in aux_copies():
            copy.wait_recv()
        own = aux_out[...].astype(F32)
        to_south, to_north, to_west, to_east = [aux_in[d].astype(F32) for d in range(4)]
        to_north = to_north * jnp.where(lat < n_lat - 1, 1.0, 0.0)
        to_south = to_south * jnp.where(lat > 0, 1.0, 0.0)
        lane = iota((16, 128), 1)
        right = jnp.where(lane == 127, pltpu.roll(to_east, 127, 1), pltpu.roll(own, 127, 1))
        left = jnp.where(lane == 0, pltpu.roll(to_west, 1, 1), pltpu.roll(own, 1, 1))
        u, v, m = own[0:4], own[4:8], own[8:12]
        ur, vr, mr = right[0:4], right[4:8], right[8:12]
        ul, vl, ml = left[0:4], left[4:8], left[8:12]
        ut = jnp.concatenate([to_south[3:4], u, to_north[0:1]], axis=0)
        vt = jnp.concatenate([to_south[7:8], v, to_north[4:5]], axis=0)
        mt = jnp.concatenate([to_south[11:12], m, to_north[8:9]], axis=0)
        fur, ful = 0.5 * (u + ur), 0.5 * (ul + u)
        oxr, oxl = m * mr, ml * m
        fv, oy = 0.5 * (vt[0:5] + vt[1:6]), mt[0:5] * mt[1:6]
        ux, vx = 0.5 * (ur - ul), 0.5 * (vr - vl)
        uy, vy = 0.5 * (ut[2:6] - ut[0:4]), 0.5 * (vt[2:6] - vt[0:4])
        wide = lambda a: jnp.broadcast_to(a, (8, 128))
        for y in range(4):
            for n, a in enumerate((fur, oxr, ful, oxl)):
                face_x[y, n] = wide(a[y : y + 1])
            sea_ref[y] = wide(m[y : y + 1])
        for y in range(5):
            face_y[y, 0] = wide(fv[y : y + 1])
            face_y[y, 1] = wide(oy[y : y + 1])
        for d in range(HALF):
            phi = (d + 1) * 2.0 * math.pi / ND
            fs, fc = math.sin(phi), math.cos(phi)
            turn = TURN_SCALE * ((fs * fc) * (ux - vy) + (fs * fs) * uy - (fc * fc) * vx)
            for y in range(4):
                turn_ref[y, d] = wide(turn[y : y + 1])

    def arrive(c):
        at, width = CHUNKS[c]
        for copy in halo_copies(c):
            copy.wait_recv()
        e_ref[0, at : at + HELD[c], :] = ns_in[c][1].astype(F32)
        e_ref[5, at : at + HELD[c], :] = ns_in[c][0].astype(F32)
        placed = dot(ew_in[c][...].reshape(32, width), place, 0, 0)
        for y in range(4):
            hp_ref[y, at : at + width, :] = placed[:, 128 * y : 128 * (y + 1)]

    lane = iota((8, 128), 1)

    def advance(step, _):
        g, y = step // 4, step % 4
        base = g * GROUP
        cg = table_ref[pl.ds(pl.multiple_of(80 + g * 8, 8), 8), :]
        fur, oxr, ful, oxl = [face_x[y, n] for n in range(4)]
        fvs, oys, fvn, oyn = face_y[y, 0], face_y[y, 1], face_y[y + 1, 0], face_y[y + 1, 1]
        sea = sea_ref[y]

        def flux(speed, here, there, is_open):
            return is_open * (speed * jnp.where(speed > 0.0, here, there))

        moved = []
        for d in range(HALF):
            theta = (d + 0.5) * 2.0 * math.pi / ND
            rows = pl.ds(base + d, 8, stride=HALF)
            here, up, down = e_ref[y + 1, rows, :], e_ref[y + 2, rows, :], e_ref[y, rows, :]
            halo = hp_ref[y, rows, :]
            right = jnp.where(lane == 127, halo, pltpu.roll(here, 127, 1))
            left = jnp.where(lane == 0, halo, pltpu.roll(here, 1, 1))
            sx, sy = cg * math.cos(theta), cg * math.sin(theta)
            div_x = flux(sx + fur, here, right, oxr) - flux(sx + ful, left, here, oxl)
            div_y = flux(sy + fvn, here, up, oyn) - flux(sy + fvs, down, here, oys)
            moved.append(here - div_x - div_y)
        half = iota((8, 128), 0) % 2
        swap = lambda a: jnp.where(half == 0, pltpu.roll(a, 7, 0), pltpu.roll(a, 1, 0))
        first = swap(moved[0])
        bent = []
        for d in range(HALF):
            turn = turn_ref[y, d]
            bent.append(turn * jnp.where(turn > 0.0, moved[d], moved[d + 1] if d + 1 < HALF else first))
        before = swap(bent[-1])
        for d in range(HALF):
            value = (moved[d] - (bent[d] - before)) * sea
            o_ref[pl.ds(g * (4 * GROUP) + d * 4 + y, 8, stride=4 * HALF), :] = value
            before = bent[d]
        return 0

    def finish(g, _):
        rows = pl.ds(pl.multiple_of(g * 4 * GROUP, 16), 4 * GROUP)
        out_ref[rows, :] = o_ref[rows, :].astype(BF16)
        return 0

    def propagate(c):
        first, last = READY_GROUPS[c]
        arrive(c)
        lax.fori_loop(first * 4, last * 4, advance, 0)
        lax.fori_loop(first, last, finish, 0)

    middle(0)
    send1(1)
    drain(cur_all.at[core], c_sem.at[1])
    swap.start()
    middle(2)
    send1(3)
    send_aux()
    middle(1)
    middle(3)
    prepare()
    pick(0)
    pick(1)
    propagate(0)
    pick(2)
    pick(3)
    propagate(1)
    propagate(2)
    propagate(3)

    for c in range(NC):
        drain(x1[c].at[pl.ds(0, SHAPES[FIRST[c]][0] - 1)], p1_send.at[c])
        drain(y2[c].at[pl.ds(0, SHAPES[1 - FIRST[c]][0] - 1)], p2_send.at[c])
        for copy in halo_copies(c):
            copy.wait_send()
    drain(cur_all.at[core, pl.ds(0, NZX - 1)], c_sem.at[0])
    swap.wait_send()
    for copy in aux_copies():
        copy.wait_send()


def tables():
    ratio = 1.1 ** np.arange(NF)
    theta = (np.arange(ND) + 0.5) * 2.0 * np.pi / ND
    table = np.zeros((232, 1))
    table[0:ND, 0] = np.cos(theta)
    table[40 : 40 + ND, 0] = np.sin(theta)
    table[80:152, 0] = np.repeat(0.53 / ratio, 2) * np.tile([1.0, -1.0], NF)
    table[152 : 152 + NF, 0] = ratio / 44.6
    table[192 : 192 + NF, 0] = ratio / ratio[-1]
    return np.repeat(table, 128, axis=1).astype(np.float32)


def body(spec_pts, wind_u, wind_v, ocean_current, block_owner, block_slot, cell_source, land_mask):
    hbm = pl.BlockSpec(memory_space=pltpu.HBM)
    per_chunk = lambda shape: [pltpu.VMEM(shape(i, w), BF16) for i, w in enumerate(WIDTHS)]
    dma = pltpu.SemaphoreType.DMA
    out = pl.pallas_call(
        kernel,
        out_shape=jax.ShapeDtypeStruct((SPEC * 4, 128), BF16),
        in_specs=[hbm] * 9,
        out_specs=pl.BlockSpec(memory_space=pltpu.VMEM),
        scratch_shapes=[
            pltpu.VMEM((NF, ND, CELLS), BF16),
            pltpu.VMEM((1, CELLS), F32),
            pltpu.VMEM((1, CELLS), F32),
            pltpu.VMEM((232, 128), F32),
            pltpu.VMEM((1, 4), jnp.int32),
            pltpu.VMEM((1, 4), jnp.int32),
            pltpu.VMEM((4, 128), jnp.int32),
            pltpu.VMEM((4, 128), jnp.int32),
            pltpu.VMEM((PAD, CELLS), F32),
            pltpu.VMEM((6, PAD, 128), F32),
            pltpu.VMEM((4, PAD, 128), F32),
            pltpu.VMEM((SPEC * 4, 128), F32),
            per_chunk(lambda i, w: (*SHAPES[FIRST[i]], w)),
            per_chunk(lambda i, w: (*SHAPES[FIRST[i]], w)),
            per_chunk(lambda i, w: (*SHAPES[1 - FIRST[i]], w)),
            per_chunk(lambda i, w: (*SHAPES[1 - FIRST[i]], w)),
            per_chunk(lambda i, w: (2, HELD[i], 128)),
            per_chunk(lambda i, w: (2, HELD[i], 128)),
            per_chunk(lambda i, w: (16, w)),
            per_chunk(lambda i, w: (2, 16, w)),
            pltpu.VMEM((2, NZX, 16, 128), BF16),
            pltpu.VMEM((16, 128), BF16),
            pltpu.VMEM((4, 16, 128), BF16),
            pltpu.VMEM((4, 4, 8, 128), F32),
            pltpu.VMEM((5, 2, 8, 128), F32),
            pltpu.VMEM((4, HALF, 8, 128), F32),
            pltpu.VMEM((4, 8, 128), F32),
            pltpu.VMEM((2, CELLS, CELLS), BF16),
            dma((NC,)), dma((NC,)), dma((NC,)), dma((NC,)), dma((NC, 4)), dma((NC, 4)), dma((4,)), dma((4,)), dma((4,)),
            dma((LOADS + 7,)),
        ],
        compiler_params=pltpu.CompilerParams(
            collective_id=0, has_side_effects=True, vmem_limit_bytes=50 * 2**20
        ),
    )(*[
        pltpu.with_memory_space_constraint(a, pltpu.HBM)
        for a in (
            spec_pts, wind_u.reshape(1, CELLS), wind_v.reshape(1, CELLS), jnp.asarray(tables()),
            ocean_current.reshape(16, 128), block_owner.T, block_slot.T, cell_source, land_mask,
        )
    ])
    return out.reshape(NF, ND, 4, 128)


def solution(mesh):
    return jax.shard_map(
        body,
        mesh=mesh,
        in_specs=(
            P(None, None, ("lon", "lat")),
            P(("lon", "lat")),
            P(("lon", "lat")),
            P(None, "lat", "lon", None),
            P("lat", "lon"),
            P("lat", "lon"),
            P("lat", "lon"),
            P("lat", "lon"),
        ),
        out_specs=P(None, None, "lat", "lon"),
        check_vma=False,
    )
```
